512 devices in a mesh: seq: 32 (over z_lo, y), tp: 16 (over z_hi, x, core).
Axes of the slice: x: 4, y: 4, z: 16 (z_hi: 2, z_lo: 8; z = z_hi * 8 + z_lo), core: 2. Of those that a mesh axis runs over, the one named last changes fastest.
Arguments:
- page_counts: int32 [32], replicated, may hold values from 1 to 4, 64 in all
- page_order: int32 [64], replicated, may hold values from 0 to 63, each once
- queries: bfloat16 [8192, 8192], P('seq', 'tp'), may hold values from -8 to 8
- keys: bfloat16 [8192, 1024], P('seq'), may hold values from -8 to 8
- values: bfloat16 [8192, 1024], P('seq'), may hold values from -6 to 6
- out_weight: bfloat16 [8192, 8192], P('tp', 'seq'), may hold values from -1 to 1
Outputs:
- mixed: bfloat16 [8192, 8192], P(('seq', 'tp'))
The draws below stay inside these ranges and needn't reach their ends.
All inputs are finite; a program needn't handle non-finite values.
Results may differ from the reference program's by a relative error of at most 0.018.
Values may be sent and summed in bfloat16 or wider, within the bound.
No kernel may reach another device: no remote copies, remote signals or barrier semaphores. Data moves between devices by JAX's collectives and lax.ppermute only.
A program may use at most 64 MiB of HBM per device.

```python
import math
import jax
import jax.numpy as jnp
import numpy as np
from jax import lax

D = 8192
HQ = 64
KVH = 8
HD = 128
PAGE = 64
SLOTS = 4
PAGES = 64
ALLROWS = 8192
N_SEQ = 32
N_TP = 16


def shared_keys(key):
    base = jax.random.normal(jax.random.fold_in(key, 11), (ALLROWS, KVH * HD), jnp.float32)
    return jnp.clip(base, -6.0, 6.0)


def draw_keys(key, part):
    base = shared_keys(key)
    return base.astype(jnp.bfloat16)


def draw_queries(key, part):
    key = jax.random.fold_in(key, 5)
    drawn = jnp.clip(jax.random.normal(key, (ALLROWS, HQ * HD), jnp.float32), -6.0, 6.0)
    return drawn.astype(jnp.bfloat16)


def shard_levels(stream_key, dims, pieces, least, high):
    factor_of, own = 1.0, jax.random.fold_in(stream_key, 6)
    for position, parts in pieces:
        draws = jnp.exp(jax.random.uniform(jax.random.fold_in(own, position), (parts,), jnp.float32, least / len(pieces), high / len(pieces)))
        factor_of = factor_of * jnp.repeat(draws, dims[position] // parts).reshape([-1 if axis == position else 1 for axis in range(len(dims))])
    return factor_of


def split_up(amount, total, bound, slope):
    portions = [(1 << 20) // math.isqrt(rank ** slope) + 1 for rank in range(2, amount + 1)]
    rest, given = total - bound - (amount - 1), [1] * (amount - 1)
    while rest > 0:
        movable = [i for i in range(amount - 1) if given[i] < bound]
        mass, left = sum([portions[i] for i in movable]), rest
        for i in movable:
            more = min(bound - given[i], max(1, left * portions[i] // mass), rest)
            given[i] = given[i] + more
            rest = rest - more
    return np.array([bound] + given)


def uneven(key, amount, total, reach, skew):
    if amount == 2:
        one = jax.random.randint(key, (), max(1, total - reach), min(reach, total - 1) + 1)
        return jnp.stack([one, total - one])
    tallies = jnp.asarray(split_up(amount, total, reach, skew), jnp.int32)
    twos = (amount - 1) // 2
    giver, taker = tallies[1:1 + 2 * twos:2], tallies[2:2 + 2 * twos:2]
    slack = jnp.minimum(giver - 1, reach - taker)
    moved = jax.random.randint(jax.random.fold_in(key, 1), (twos,), 0, 1 << 20) % (slack + 1)
    tallies = tallies.at[1:1 + 2 * twos:2].set(giver - moved).at[2:2 + 2 * twos:2].set(taker + moved)
    return tallies[jax.random.permutation(jax.random.fold_in(key, 2), amount)]


def normal_values(key, shape, scale, reach, shards=(), kind=jnp.bfloat16):
    gain = shard_levels(key, shape, shards, -0.22, 0.18) if shards else 1.0
    array = jax.random.normal(key, shape, jnp.float32) * scale * gain
    return jnp.minimum(jnp.maximum(array, -reach), reach).astype(kind)


def setup_inputs(seed: int = 0) -> dict:
    splits = jax.random.split(jax.random.key(seed), 7)
    page_counts = uneven(splits[0], N_SEQ, PAGES, SLOTS, 2).astype(jnp.int32)
    page_order = jax.random.permutation(splits[1], PAGES).astype(jnp.int32)
    queries = draw_queries(jax.random.fold_in(splits[6], 71), 0)
    keys = draw_keys(jax.random.fold_in(splits[6], 71), 0)
    values = normal_values(splits[4], (ALLROWS, KVH * HD), 1.0, 6.0, ((0, 32),))
    out_weight = normal_values(splits[5], (HQ * HD, D), (HQ * HD // 256) ** -0.5, 1.0, ((0, 16), (1, 32)))
    return dict(page_counts=page_counts, page_order=page_order, queries=queries, keys=keys, values=values, out_weight=out_weight)


def slot_positions(page_counts, page_order):
    slot_ids = jnp.arange(N_SEQ * SLOTS, dtype=jnp.int32)
    owner = slot_ids // SLOTS
    local = slot_ids % SLOTS
    before = (jnp.cumsum(page_counts) - page_counts).astype(jnp.int32)
    rank = before[owner] + local
    live = local < page_counts[owner]
    rank = jnp.clip(rank, 0, PAGES - 1).astype(jnp.int32)
    page = page_order[rank]
    offsets = jnp.arange(PAGE, dtype=jnp.int32)
    pos = (page[:, None] * PAGE + offsets[None, :]).reshape(-1)
    live_rows = jnp.repeat(live, PAGE)
    return pos, live_rows


def reference(page_counts, page_order, queries, keys, values, out_weight):
    pos, live = slot_positions(page_counts, page_order)
    group = HQ // KVH
    scale = HD ** -0.5
    visible = live[None, :] & (pos[None, :] <= pos[:, None])
    denom_mask = live

    def one_head(head):
        kv = head // group
        q = lax.dynamic_slice_in_dim(queries, head * HD, HD, 1)
        k = lax.dynamic_slice_in_dim(keys, kv * HD, HD, 1)
        v = lax.dynamic_slice_in_dim(values, kv * HD, HD, 1)
        s = jnp.dot(q, k.T, preferred_element_type=jnp.float32) * scale
        s = jnp.where(visible, s, jnp.float32(-1e30))
        best = jnp.max(s, axis=1, keepdims=True)
        p = jnp.where(visible, jnp.exp(s - best), jnp.float32(0.0))
        total = jnp.sum(p, axis=1)
        out = jnp.dot(p.astype(jnp.bfloat16), v, preferred_element_type=jnp.float32)
        out = out / jnp.where(denom_mask, total, jnp.float32(1.0))[:, None]
        return jnp.where(denom_mask[:, None], out, jnp.float32(0.0)).astype(jnp.bfloat16)

    heads = lax.map(one_head, jnp.arange(HQ, dtype=jnp.int32))
    attention = jnp.transpose(heads, (1, 0, 2)).reshape(ALLROWS, HQ * HD)
    width = HQ * HD // N_TP

    def add_part(total, index):
        block = lax.dynamic_slice_in_dim(attention, index * width, width, 1)
        rows = lax.dynamic_slice_in_dim(out_weight, index * width, width, 0)
        part = lax.optimization_barrier(jnp.dot(block, rows, preferred_element_type=jnp.float32).astype(jnp.bfloat16))
        return total + part.astype(jnp.float32), None

    summed, _ = lax.scan(add_part, jnp.zeros((ALLROWS, D), jnp.float32), jnp.arange(N_TP, dtype=jnp.int32))
    return summed.astype(jnp.bfloat16)
```

```python
import jax
import jax.numpy as jnp
from jax import lax
from jax.experimental import pallas as pl
from jax.experimental.pallas import tpu as pltpu
from jax.sharding import Mesh, PartitionSpec as P

HD = 128
PAGE = 64
SLOTS = 4
PAGES = 64
HEADS = 4
ZL, Y, ZH, X, C = 8, 4, 2, 4, 2
N_SEQ = ZL * Y
ROWS = SLOTS * PAGE
CHUNK = 512
SCALE = HD**-0.5


def attention_kernel(counts, order, place, q_ref, own_ref, other_ref, o_ref, k_sc, v_sc):
    me = place[0]
    core = place[1]

    def sort_pages(k_ref, v_ref):
        def one(d, rank):
            held = counts[d]
            base = ((d % Y) * ZL + d // Y) * ROWS
            for j in range(SLOTS):

                @pl.when(j < held)
                def _():
                    to = pl.multiple_of(order[rank + j] * PAGE, PAGE)
                    at = pl.multiple_of(base + j * PAGE, PAGE)
                    k_sc[pl.ds(to, PAGE), :] = k_ref[pl.ds(at, PAGE), :]
                    v_sc[pl.ds(to, PAGE), :] = v_ref[pl.ds(at, PAGE), :]

            return rank + held

        lax.fori_loop(0, N_SEQ, one, jnp.int32(0))

    @pl.when(core == 0)
    def _():
        sort_pages(own_ref, other_ref)

    @pl.when(core == 1)
    def _():
        sort_pages(other_ref, own_ref)

    before = lax.fori_loop(0, me, lambda d, s: s + counts[d], jnp.int32(0))
    live = counts[me]

    def store(j, rows):
        for b in range(2):
            to = (2 * (j % 2) + b) * 64 + (j // 2) * 32
            for h in range(HEADS):
                o_ref[to : to + 32, h * HD : (h + 1) * HD] = rows(h, b)

    for j in range(SLOTS):

        @pl.when(j < live)
        def _():
            page = order[before + j]
            q = jnp.concatenate(
                [q_ref[j * PAGE : (j + 1) * PAGE, h * HD : (h + 1) * HD] for h in range(HEADS)], axis=0
            )

            def step(i, state, last):
                best, total, accum = state
                at = pl.multiple_of(i * CHUNK, CHUNK)
                k = k_sc[pl.ds(at, CHUNK), :]
                v = v_sc[pl.ds(at, CHUNK), :]
                s = lax.dot_general(q, k, (((1,), (1,)), ((), ())), preferred_element_type=jnp.float32)
                if last:
                    row = lax.broadcasted_iota(jnp.int32, s.shape, 0) % PAGE + page * PAGE
                    col = lax.broadcasted_iota(jnp.int32, s.shape, 1) + at
                    s = jnp.where(col <= row, s, jnp.float32(-1e30))
                new = jnp.maximum(best, jnp.max(s, axis=1, keepdims=True))
                p = jnp.exp((s - new) * SCALE)
                fade = jnp.exp((best - new) * SCALE)
                total = total * fade + jnp.sum(p, axis=1, keepdims=True)
                accum = accum * fade + jnp.dot(p.astype(jnp.bfloat16), v, preferred_element_type=jnp.float32)
                return new, total, accum

            state = (
                jnp.full((HEADS * PAGE, 1), -1e30, jnp.float32),
                jnp.zeros((HEADS * PAGE, 1), jnp.float32),
                jnp.zeros((HEADS * PAGE, HD), jnp.float32),
            )
            full = page // (CHUNK // PAGE)
            state = lax.fori_loop(0, full, lambda i, s: step(i, s, False), state)
            _, total, accum = step(full, state, True)
            out = (accum / total).astype(jnp.bfloat16)
            store(j, lambda h, b: out[h * PAGE + b * 32 : h * PAGE + b * 32 + 32, :])

        @pl.when(j >= live)
        def _():
            store(j, lambda h, b: jnp.zeros((32, HD), jnp.bfloat16))


def attend(counts, order, place, q, own, other):
    smem = pl.BlockSpec(memory_space=pltpu.SMEM)
    vmem = pl.BlockSpec(memory_space=pltpu.VMEM)
    return pl.pallas_call(
        attention_kernel,
        out_shape=jax.ShapeDtypeStruct(q.shape, jnp.bfloat16),
        in_specs=[smem, smem, smem, vmem, vmem, vmem],
        out_specs=vmem,
        scratch_shapes=[pltpu.VMEM((PAGES * PAGE, HD), jnp.bfloat16) for _ in range(2)],
        compiler_params=pltpu.CompilerParams(vmem_limit_bytes=40 << 20),
    )(counts, order, place, q, own, other)


def project_kernel(a_ref, b_ref, w_ref, o_ref):
    half = a_ref.shape[2]
    part = jnp.dot(a_ref[0], w_ref[:half, :], preferred_element_type=jnp.float32)
    part += jnp.dot(b_ref[0], w_ref[half:, :], preferred_element_type=jnp.float32)
    o_ref[...] = part.astype(jnp.bfloat16).reshape(o_ref.shape)


def project(a, b, w):
    n = w.shape[1]
    return pl.pallas_call(
        project_kernel,
        grid=(Y,),
        out_shape=jax.ShapeDtypeStruct((X, Y, ROWS // X, n), jnp.bfloat16),
        in_specs=[
            pl.BlockSpec((1, ROWS, a.shape[2]), lambda i: (i, 0, 0)),
            pl.BlockSpec((1, ROWS, a.shape[2]), lambda i: (i, 0, 0)),
            pl.BlockSpec(w.shape, lambda i: (0, 0)),
        ],
        out_specs=pl.BlockSpec((X, 1, ROWS // X, n), lambda i: (0, i, 0, 0)),
        compiler_params=pltpu.CompilerParams(vmem_limit_bytes=40 << 20),
    )(a, b, w)


def spread(piece, axis, count):
    return lax.all_to_all(jnp.broadcast_to(piece[None], (count, *piece.shape)), axis, 0, 0)


def swap(piece, axis):
    return lax.ppermute(piece, axis, [(0, 1), (1, 0)])


def body(counts, order, queries, keys, values, weight):
    zl, y, zh, x, c = (lax.axis_index(name) for name in ("zl", "y", "zh", "x", "c"))
    with jax.named_scope("weight_gather"):
        given = swap(lax.dynamic_slice_in_dim(weight, (1 - c) * 128, 128, 1), "c")
        kept = lax.dynamic_slice_in_dim(weight, c * 128, 128, 1)
        wide = lax.all_gather(jnp.concatenate([kept, given], axis=0), "zl", axis=1, tiled=True)
    with jax.named_scope("cache_gather"):
        head = (zh * X + x) * HD
        piece = jnp.where(
            c == 0,
            lax.dynamic_slice_in_dim(keys, head, HD, 1),
            lax.dynamic_slice_in_dim(values, head, HD, 1),
        )
        own = spread(piece, "zl", ZL).reshape(ZL * ROWS, HD)
        own = spread(own, "y", Y).reshape(N_SEQ * ROWS, HD)
        other = swap(own, "c")
    with jax.named_scope("attention"):
        place = jnp.stack([zl * Y + y, c]).astype(jnp.int32)
        heads = attend(counts, order, place, queries, own, other)
    with jax.named_scope("rows_gather"):
        mine = spread(heads, "y", Y)
        theirs = swap(mine, "c")
    with jax.named_scope("projection"):
        parts = project(mine, theirs, wide)
    with jax.named_scope("sum_x"):
        parts = lax.all_to_all(parts, "x", 0, 0)
        total = jnp.sum(parts.astype(jnp.float32), axis=0).reshape(Y, ZH, 32, ZL * 128)
    with jax.named_scope("sum_zh"):
        away = lax.dynamic_slice_in_dim(total, 1 - zh, 1, 1).astype(jnp.bfloat16)
        stay = lax.dynamic_slice_in_dim(total, zh, 1, 1)
        mixed = (stay + swap(away, "zh").astype(jnp.float32)).astype(jnp.bfloat16)
    with jax.named_scope("columns"):
        mixed = lax.all_to_all(mixed.reshape(Y * C, 16, ZL * 128), ("y", "c"), 0, 0)
        mixed = mixed.reshape(Y, C, 16, ZL, 128).transpose(2, 3, 0, 1, 4)
    return mixed.reshape(16, N_SEQ * 256)


def solution(mesh):
    fine = Mesh(mesh.devices.reshape(ZL, Y, ZH, X, C), ("zl", "y", "zh", "x", "c"))
    seq, tp = ("zl", "y"), ("zh", "x", "c")
    return jax.shard_map(
        body,
        mesh=fine,
        in_specs=(P(), P(), P(seq, tp), P(seq, None), P(seq, None), P(tp, seq)),
        out_specs=P((*seq, *tp), None),
        check_vma=False,
    )
```

```python
import jax
import jax.numpy as jnp
from jax import lax
from jax.experimental import pallas as pl
from jax.experimental.pallas import tpu as pltpu
from jax.sharding import Mesh, PartitionSpec as P

HD = 128
PAGE = 64
SLOTS = 4
PAGES = 64
HEADS = 4
ZP, ZQ, Y, ZH, X, C = 4, 2, 4, 2, 4, 2
ZL = ZP * ZQ
N_SEQ = ZL * Y
ROWS = SLOTS * PAGE
CHUNK = 512
SCALE = HD**-0.5


def attention_kernel(counts, order, place, q_ref, *refs):
    own_refs, other_refs = refs[:Y], refs[Y : 2 * Y]
    o_ref, k_sc, v_sc = refs[2 * Y :]
    me = place[0]
    core = place[1]
    my_y = me % Y
    my_q = (me // Y) % ZQ

    def sort_pages(k_refs, v_refs):
        def one(z, rank):
            base = (((z + my_q) % ZQ) * ZP + z // ZQ) * ROWS
            for col in range(Y):
                held = counts[z * Y + col]
                for shift in range(Y):

                    @pl.when((my_y + shift) % Y == col)
                    def _():
                        for j in range(SLOTS):

                            @pl.when(j < held)
                            def _():
                                to = pl.multiple_of(order[rank + j] * PAGE, PAGE)
                                at = pl.multiple_of(base + j * PAGE, PAGE)
                                k_sc[pl.ds(to, PAGE), :] = k_refs[shift][pl.ds(at, PAGE), :]
                                v_sc[pl.ds(to, PAGE), :] = v_refs[shift][pl.ds(at, PAGE), :]

                rank = rank + held
            return rank

        lax.fori_loop(0, ZL, one, jnp.int32(0))

    @pl.when(core == 0)
    def _():
        sort_pages(own_refs, other_refs)

    @pl.when(core == 1)
    def _():
        sort_pages(other_refs, own_refs)

    before = lax.fori_loop(0, me, lambda d, s: s + counts[d], jnp.int32(0))
    live = counts[me]

    def store(j, rows):
        for b in range(2):
            to = (2 * (j % 2) + b) * 64 + (j // 2) * 32
            for h in range(HEADS):
                o_ref[to : to + 32, h * HD : (h + 1) * HD] = rows(h, b)

    for j in range(SLOTS):

        @pl.when(j < live)
        def _():
            page = order[before + j]
            q = jnp.concatenate(
                [q_ref[j * PAGE : (j + 1) * PAGE, h * HD : (h + 1) * HD] for h in range(HEADS)], axis=0
            )

            def step(i, state, last):
                best, total, accum = state
                at = pl.multiple_of(i * CHUNK, CHUNK)
                k = k_sc[pl.ds(at, CHUNK), :]
                v = v_sc[pl.ds(at, CHUNK), :]
                s = lax.dot_general(q, k, (((1,), (1,)), ((), ())), preferred_element_type=jnp.float32)
                if last:
                    row = lax.broadcasted_iota(jnp.int32, s.shape, 0) % PAGE + page * PAGE
                    col = lax.broadcasted_iota(jnp.int32, s.shape, 1) + at
                    s = jnp.where(col <= row, s, jnp.float32(-1e30))
                new = jnp.maximum(best, jnp.max(s, axis=1, keepdims=True))
                p = jnp.exp((s - new) * SCALE)
                fade = jnp.exp((best - new) * SCALE)
                total = total * fade + jnp.sum(p, axis=1, keepdims=True)
                accum = accum * fade + jnp.dot(p.astype(jnp.bfloat16), v, preferred_element_type=jnp.float32)
                return new, total, accum

            state = (
                jnp.full((HEADS * PAGE, 1), -1e30, jnp.float32),
                jnp.zeros((HEADS * PAGE, 1), jnp.float32),
                jnp.zeros((HEADS * PAGE, HD), jnp.float32),
            )
            full = page // (CHUNK // PAGE)
            state = lax.fori_loop(0, full, lambda i, s: step(i, s, False), state)
            _, total, accum = step(full, state, True)
            out = (accum / total).astype(jnp.bfloat16)
            store(j, lambda h, b: out[h * PAGE + b * 32 : h * PAGE + b * 32 + 32, :])

        @pl.when(j >= live)
        def _():
            store(j, lambda h, b: jnp.zeros((32, HD), jnp.bfloat16))


def attend(counts, order, place, q, own, other):
    smem = pl.BlockSpec(memory_space=pltpu.SMEM)
    vmem = pl.BlockSpec(memory_space=pltpu.VMEM)
    return pl.pallas_call(
        attention_kernel,
        out_shape=jax.ShapeDtypeStruct(q.shape, jnp.bfloat16),
        in_specs=[smem, smem, smem, vmem] + [vmem] * (2 * Y),
        out_specs=vmem,
        scratch_shapes=[pltpu.VMEM((PAGES * PAGE, HD), jnp.bfloat16) for _ in range(2)],
        compiler_params=pltpu.CompilerParams(vmem_limit_bytes=40 << 20),
    )(counts, order, place, q, *own, *other)


def project_kernel(a_ref, b_ref, w_ref, o_ref):
    half = a_ref.shape[2]
    part = jnp.dot(a_ref[0], w_ref[:half, :], preferred_element_type=jnp.float32)
    part += jnp.dot(b_ref[0], w_ref[half:, :], preferred_element_type=jnp.float32)
    o_ref[...] = part.astype(jnp.bfloat16).reshape(o_ref.shape)


def project(a, b, w):
    n = w.shape[1]
    return pl.pallas_call(
        project_kernel,
        grid=(Y,),
        out_shape=jax.ShapeDtypeStruct((X, Y, ROWS // X, n), jnp.bfloat16),
        in_specs=[
            pl.BlockSpec((1, ROWS, a.shape[2]), lambda i: (i, 0, 0)),
            pl.BlockSpec((1, ROWS, a.shape[2]), lambda i: (i, 0, 0)),
            pl.BlockSpec(w.shape, lambda i: (0, 0)),
        ],
        out_specs=pl.BlockSpec((X, 1, ROWS // X, n), lambda i: (0, i, 0, 0)),
        compiler_params=pltpu.CompilerParams(vmem_limit_bytes=40 << 20),
    )(a, b, w)


def spread(piece, axis, count):
    return lax.all_to_all(jnp.broadcast_to(piece[None], (count, *piece.shape)), axis, 0, 0)


def swap(piece, axis):
    return lax.ppermute(piece, axis, [(0, 1), (1, 0)])


def from_next(piece, axis, count, shift):
    return lax.ppermute(piece, axis, [((i + shift) % count, i) for i in range(count)])


def body(counts, order, queries, keys, values, weight):
    zp, zq, y, zh, x, c = (lax.axis_index(name) for name in ("zp", "zq", "y", "zh", "x", "c"))
    with jax.named_scope("weight_gather"):
        given = swap(lax.dynamic_slice_in_dim(weight, (1 - c) * 128, 128, 1), "c")
        kept = lax.dynamic_slice_in_dim(weight, c * 128, 128, 1)
        narrow = jnp.concatenate([kept, given], axis=0)
    with jax.named_scope("cache_gather"):
        head = (zh * X + x) * HD
        piece = jnp.where(
            c == 0,
            lax.dynamic_slice_in_dim(keys, head, HD, 1),
            lax.dynamic_slice_in_dim(values, head, HD, 1),
        )
        narrow, piece = lax.optimization_barrier((narrow, piece))
        wide = lax.all_gather(narrow, ("zp", "zq"), axis=1, tiled=True)
        near = spread(piece, "zp", ZP)
        near = jnp.concatenate([near, swap(near, "zq")], axis=0).reshape(ZL * ROWS, HD)
        own = [near] + [from_next(near, "y", Y, shift) for shift in range(1, Y)]
        other = [swap(one, "c") for one in own]
    with jax.named_scope("attention"):
        place = jnp.stack([(zp * ZQ + zq) * Y + y, c]).astype(jnp.int32)
        heads = attend(counts, order, place, queries, own, other)
        heads, wide = lax.optimization_barrier((heads, wide))
    with jax.named_scope("rows_gather"):
        mine = spread(heads, "y", Y)
        theirs = swap(mine, "c")
    with jax.named_scope("projection"):
        parts = project(mine, theirs, wide)
    with jax.named_scope("sum_x"):
        parts = lax.all_to_all(parts, "x", 0, 0)
        total = jnp.sum(parts.astype(jnp.float32), axis=0).reshape(Y, ZH, 32, ZL * 128)
    with jax.named_scope("sum_zh"):
        away = lax.dynamic_slice_in_dim(total, 1 - zh, 1, 1).astype(jnp.bfloat16)
        stay = lax.dynamic_slice_in_dim(total, zh, 1, 1)
        mixed = (stay + swap(away, "zh").astype(jnp.float32)).astype(jnp.bfloat16)
    with jax.named_scope("columns"):
        mixed = lax.all_to_all(mixed.reshape(Y * C, 16, ZL * 128), ("y", "c"), 0, 0)
        mixed = mixed.reshape(Y, C, 16, ZL, 128).transpose(2, 3, 0, 1, 4)
    return mixed.reshape(16, N_SEQ * 256)


def solution(mesh):
    fine = Mesh(mesh.devices.reshape(ZP, ZQ, Y, ZH, X, C), ("zp", "zq", "y", "zh", "x", "c"))
    seq, tp = ("zp", "zq", "y"), ("zh", "x", "c")
    return jax.shard_map(
        body,
        mesh=fine,
        in_specs=(P(), P(), P(seq, tp), P(seq, None), P(seq, None), P(tp, seq)),
        out_specs=P((*seq, *tp), None),
        check_vma=False,
    )
```

```python
import jax
import jax.numpy as jnp
from jax import lax
from jax.experimental import pallas as pl
from jax.experimental.pallas import tpu as pltpu
from jax.sharding import Mesh, PartitionSpec as P

HD = 128
PAGE = 64
SLOTS = 4
PAGES = 64
HEADS = 4
ZA, ZB, ZQ, Y, ZH, X, C = 2, 2, 2, 4, 2, 4, 2
ZL, QUAD = ZA * ZB * ZQ, ZB * ZQ
Z = ZH * ZL
LINE = ("za", "zb", "zq", "zh", "c")
N_SEQ = ZL * Y
ROWS = SLOTS * PAGE
CHUNK = 512
SCALE = HD**-0.5


def attention_kernel(counts, order, place, q_ref, own_ref, other_ref, o_ref, k_sc, v_sc):
    me = place[0]
    core = place[1]
    my_zh = place[2]
    my_z = me // Y

    def sort_pages(k_ref, v_ref):
        def one(d, rank):
            held = counts[d]
            z = d // Y
            far = (z + my_z) % 2
            near = my_z + far * (1 - 2 * (my_z % 2))
            base = ((d % Y) * ZL + far * (ZL // 2) + (z - near + ZL) % ZL // 2) * ROWS
            for j in range(SLOTS):

                @pl.when(j < held)
                def _():
                    to = pl.multiple_of(order[rank + j] * PAGE, PAGE)
                    at = pl.multiple_of(base + j * PAGE, PAGE)
                    k_sc[pl.ds(to, PAGE), :] = k_ref[pl.ds(at, PAGE), :]
                    v_sc[pl.ds(to, PAGE), :] = v_ref[pl.ds(at, PAGE), :]

            return rank + held

        lax.fori_loop(0, N_SEQ, one, jnp.int32(0))

    @pl.when(core == 0)
    def _():
        sort_pages(own_ref, other_ref)

    @pl.when(core == 1)
    def _():
        sort_pages(other_ref, own_ref)

    before = lax.fori_loop(0, me, lambda d, s: s + counts[d], jnp.int32(0))
    live = counts[me]

    def store(j, rows):
        kept = (my_zh == j // 2).astype(jnp.int32)
        for b in range(2):
            for h in range(HEADS):
                o_ref[kept, 2 * (j % 2) + b, :, h * HD : (h + 1) * HD] = rows(h, b)

    for j in range(SLOTS):

        @pl.when(j < live)
        def _():
            page = order[before + j]
            q = jnp.concatenate(
                [q_ref[j * PAGE : (j + 1) * PAGE, h * HD : (h + 1) * HD] for h in range(HEADS)], axis=0
            )

            def step(i, state, last):
                best, total, accum = state
                at = pl.multiple_of(i * CHUNK, CHUNK)
                k = k_sc[pl.ds(at, CHUNK), :]
                v = v_sc[pl.ds(at, CHUNK), :]
                s = lax.dot_general(q, k, (((1,), (1,)), ((), ())), preferred_element_type=jnp.float32)
                if last:
                    row = lax.broadcasted_iota(jnp.int32, s.shape, 0) % PAGE + page * PAGE
                    col = lax.broadcasted_iota(jnp.int32, s.shape, 1) + at
                    s = jnp.where(col <= row, s, jnp.float32(-1e30))
                new = jnp.maximum(best, jnp.max(s, axis=1, keepdims=True))
                p = jnp.exp((s - new) * SCALE)
                fade = jnp.exp((best - new) * SCALE)
                total = total * fade + jnp.sum(p, axis=1, keepdims=True)
                accum = accum * fade + jnp.dot(p.astype(jnp.bfloat16), v, preferred_element_type=jnp.float32)
                return new, total, accum

            state = (
                jnp.full((HEADS * PAGE, 1), -1e30, jnp.float32),
                jnp.zeros((HEADS * PAGE, 1), jnp.float32),
                jnp.zeros((HEADS * PAGE, HD), jnp.float32),
            )
            full = page // (CHUNK // PAGE)
            state = lax.fori_loop(0, full, lambda i, s: step(i, s, False), state)
            _, total, accum = step(full, state, True)
            out = (accum / total).astype(jnp.bfloat16)
            store(j, lambda h, b: out[h * PAGE + b * 32 : h * PAGE + b * 32 + 32, :])

        @pl.when(j >= live)
        def _():
            store(j, lambda h, b: jnp.zeros((32, HD), jnp.bfloat16))


def attend(counts, order, place, q, own, other):
    smem = pl.BlockSpec(memory_space=pltpu.SMEM)
    vmem = pl.BlockSpec(memory_space=pltpu.VMEM)
    return pl.pallas_call(
        attention_kernel,
        out_shape=jax.ShapeDtypeStruct((ZH, X, 32, HEADS * HD), jnp.bfloat16),
        in_specs=[smem, smem, smem, vmem, vmem, vmem],
        out_specs=vmem,
        scratch_shapes=[pltpu.VMEM((PAGES * PAGE, HD), jnp.bfloat16) for _ in range(2)],
        compiler_params=pltpu.CompilerParams(vmem_limit_bytes=40 << 20),
    )(counts, order, place, q, own, other)


def project_kernel(me, a_ref, b_ref, w_ref, o_ref):
    half = a_ref.shape[-1]
    w = jnp.concatenate([w_ref[0, 0], w_ref[0, 1]], axis=1)
    part = jnp.dot(a_ref[...].reshape(-1, half), w[:half], preferred_element_type=jnp.float32)
    part += jnp.dot(b_ref[...].reshape(-1, half), w[half:], preferred_element_type=jnp.float32)
    part = part.astype(jnp.bfloat16).reshape(QUAD, X, 32, 2 * HD)
    for i in range(QUAD):
        o_ref[:, me[0] ^ i] = part[i]


def project(me, a, b, w):
    rows = pl.BlockSpec(a.shape, lambda i: (0, 0, 0, 0))
    return pl.pallas_call(
        project_kernel,
        grid=(Y,),
        out_shape=jax.ShapeDtypeStruct((X, QUAD, 32, ZL * HD), jnp.bfloat16),
        in_specs=[pl.BlockSpec(memory_space=pltpu.SMEM), rows, rows, pl.BlockSpec((1, *w.shape[1:]), lambda i: (i, 0, 0, 0))],
        out_specs=pl.BlockSpec((X, QUAD, 32, 2 * HD), lambda i: (0, 0, 0, i)),
        compiler_params=pltpu.CompilerParams(vmem_limit_bytes=24 << 20),
    )(me, a, b, w)


def spread(piece, axis, count):
    return lax.all_to_all(jnp.broadcast_to(piece[None], (count, *piece.shape)), axis, 0, 0)


def swap(piece, axis):
    return lax.ppermute(piece, axis, [(0, 1), (1, 0)])


def quad(piece, step):
    return lax.ppermute(piece, ("zb", "zq"), [(i, i ^ step) for i in range(QUAD)])


def along(piece, step):
    def place(z, c):
        return ((z % ZL) * ZH + z // ZL) * C + c

    perm = [(place(z, c), place((z + step(z, c)) % Z, c)) for z in range(Z) for c in range(C)]
    return lax.ppermute(piece, LINE, perm)


def body(counts, order, queries, keys, values, weight):
    za, zb, zq, y, zh, x, c = (lax.axis_index(name) for name in ("za", "zb", "zq", "y", "zh", "x", "c"))
    zl = (za * ZB + zb) * ZQ + zq

    def piece(step):
        owner = (zh * ZL + zl + step + Z) % Z // ZL
        head = (owner * X + x) * HD
        return jnp.where(
            c == 0,
            lax.dynamic_slice_in_dim(keys, head, HD, 1),
            lax.dynamic_slice_in_dim(values, head, HD, 1),
        )

    with jax.named_scope("cache_gather"):
        near = [
            piece(0),
            along(piece(-2), lambda z, c: -2),
            along(piece(8 * c - 4), lambda z, c: 8 * c - 4),
            along(piece(2), lambda z, c: 2),
        ]
        near, weight = lax.optimization_barrier((near, weight))
        near = jnp.concatenate(near, axis=0)
        near = jnp.concatenate([near, swap(near, "zq")], axis=0)
    with jax.named_scope("weight_gather"):
        given = swap(lax.dynamic_slice_in_dim(weight, (1 - c) * HD, HD, 1), "c")
        kept = lax.dynamic_slice_in_dim(weight, c * HD, HD, 1)
        narrow = jnp.concatenate([kept, given], axis=0)
        near, narrow = lax.optimization_barrier((near, narrow))
        facing = swap(narrow, "za")
    with jax.named_scope("cache_gather"):
        own = spread(near, "y", Y).reshape(N_SEQ * ROWS, HD)
        own, narrow, facing = lax.optimization_barrier((own, narrow, facing))
        other = swap(own, "c")
    with jax.named_scope("weight_gather"):
        wide = jnp.stack([jnp.where(za == 0, narrow, facing), jnp.where(za == 0, facing, narrow)])
        wide = spread(wide, "y", Y)
    with jax.named_scope("attention"):
        place = jnp.stack([zl * Y + y, c, zh]).astype(jnp.int32)
        heads = attend(counts, order, place, queries, own, other)

    def sum_x(mine, wide):
        with jax.named_scope("rows_gather"):
            theirs = swap(mine, "c")
        with jax.named_scope("projection"):
            here = jnp.reshape(zb * ZQ + zq, (1,)).astype(jnp.int32)
            parts = project(here, mine, theirs, wide)
        with jax.named_scope("sum_x"):
            parts = lax.all_to_all(parts, "x", 0, 0)
            return jnp.sum(parts.astype(jnp.float32), axis=0)

    with jax.named_scope("rows_gather"):
        first, second = (jnp.stack([rows] + [quad(rows, step) for step in range(1, QUAD)]) for rows in heads)
        first, wide = lax.optimization_barrier((first, wide))
    away = sum_x(first, wide)
    with jax.named_scope("sum_zh"):
        away, second = lax.optimization_barrier((away.astype(jnp.bfloat16), second))
        back = swap(away, "zh")
    stay = sum_x(second, wide)
    with jax.named_scope("columns"):
        mixed = (stay + back.astype(jnp.float32)).astype(jnp.bfloat16)
        mixed = lax.all_to_all(mixed.reshape(QUAD * C, 16, ZL * HD), ("zb", "zq", "c"), 0, 0)
        mixed = mixed.reshape(ZB, ZQ, C, 16, Y, ZA, HD).transpose(3, 5, 0, 1, 4, 2, 6)
    return mixed.reshape(16, N_SEQ * 256)


def solution(mesh):
    fine = Mesh(mesh.devices.reshape(ZA, ZB, ZQ, Y, ZH, X, C), ("za", "zb", "zq", "y", "zh", "x", "c"))
    seq, tp = ("za", "zb", "zq", "y"), ("zh", "x", "c")
    return jax.shard_map(
        body,
        mesh=fine,
        in_specs=(P(), P(), P(seq, tp), P(seq, None), P(seq, None), P(tp, seq)),
        out_specs=P((*seq, *tp), None),
        check_vma=False,
    )
```

```python
import math

import jax
import jax.numpy as jnp
from jax import lax
from jax.experimental import pallas as pl
from jax.experimental.pallas import tpu as pltpu
from jax.sharding import Mesh, PartitionSpec as P

HD = 128
PAGE = 64
SLOTS = 4
PAGES = 64
HEADS = 4
ZA, ZB, ZQ, Y, ZH, X, C = 2, 2, 2, 4, 2, 4, 2
ZL, QUAD = ZA * ZB * ZQ, ZB * ZQ
Z = ZH * ZL
LINE = ("za", "zb", "zq", "zh", "c")
N_SEQ = ZL * Y
ROWS = SLOTS * PAGE
CHUNK = 2048
SCALE = HD**-0.5 * math.log2(math.e)


def attention_kernel(counts, order, place, q_ref, own_ref, other_ref, o_ref, k_sc, v_sc):
    me = place[0]
    core = place[1]
    my_zh = place[2]
    my_z = me // Y

    def sort_pages(k_ref, v_ref):
        def one(rank, at):
            d, j = at
            z = d // Y
            far = (z + my_z) % 2
            near = my_z + far * (1 - 2 * (my_z % 2))
            base = (d % Y) * ZL + far * (ZL // 2) + (z - near + ZL) % ZL // 2
            src = pl.multiple_of(base * ROWS + j * PAGE, PAGE)
            to = pl.multiple_of(order[rank] * PAGE, PAGE)
            k_sc[pl.ds(to, PAGE), :] = k_ref[pl.ds(src, PAGE), :]
            v_sc[pl.ds(to, PAGE), :] = v_ref[pl.ds(src, PAGE), :]
            last = j + 1 >= counts[d]
            return jnp.where(last, jnp.minimum(d + 1, N_SEQ - 1), d), jnp.where(last, 0, j + 1)

        lax.fori_loop(0, PAGES, one, (jnp.int32(0), jnp.int32(0)), unroll=4)

    @pl.when(core == 0)
    def _():
        sort_pages(own_ref, other_ref)

    @pl.when(core == 1)
    def _():
        sort_pages(other_ref, own_ref)

    before = lax.fori_loop(0, me, lambda d, s: s + counts[d], jnp.int32(0))
    live = counts[me]

    def store(j, rows):
        kept = (my_zh == j // 2).astype(jnp.int32)
        for b in range(2):
            for h in range(HEADS):
                o_ref[kept, 2 * (j % 2) + b, :, h * HD : (h + 1) * HD] = rows(h, b)

    for j in range(SLOTS):

        @pl.when(j < live)
        def _():
            page = order[before + j]
            groups = 1
            count = HEADS // groups
            q = [
                jnp.concatenate(
                    [q_ref[j * PAGE : (j + 1) * PAGE, h * HD : (h + 1) * HD] for h in range(g * count, (g + 1) * count)],
                    axis=0,
                )
                for g in range(groups)
            ]
            size = count * PAGE

            def step(at, state, last, CHUNK):
                k = k_sc[pl.ds(at, CHUNK), :]
                v = v_sc[pl.ds(at, CHUNK), :]
                if last:
                    row = lax.broadcasted_iota(jnp.int32, (size, CHUNK), 0) % PAGE + page * PAGE
                    seen = lax.broadcasted_iota(jnp.int32, (size, CHUNK), 1) + at <= row
                out = []
                for g in range(groups):
                    best, total, accum = state[g]
                    s = lax.dot_general(q[g], k, (((1,), (1,)), ((), ())), preferred_element_type=jnp.float32)
                    if last:
                        s = jnp.where(seen, s, jnp.float32(-1e30))
                    new = jnp.maximum(best, jnp.max(s, axis=1, keepdims=True))
                    p = jnp.exp2((s - new) * SCALE)
                    fade = jnp.exp2((best - new) * SCALE)
                    total = total * fade + jnp.sum(p, axis=1, keepdims=True)
                    accum = accum * fade + jnp.dot(p.astype(jnp.bfloat16), v, preferred_element_type=jnp.float32)
                    out.append((new, total, accum))
                return tuple(out)

            state = tuple(
                (
                    jnp.full((size, 1), -1e30, jnp.float32),
                    jnp.zeros((size, 1), jnp.float32),
                    jnp.zeros((size, HD), jnp.float32),
                )
                for _ in range(groups)
            )
            full = page // (CHUNK // PAGE)
            state = lax.fori_loop(
                0, full, lambda i, s: step(pl.multiple_of(i * CHUNK, CHUNK), s, False, CHUNK), state
            )
            rest = pl.multiple_of(full * CHUNK, CHUNK)
            state = lax.cond(
                page % (CHUNK // PAGE) < CHUNK // PAGE // 2,
                lambda s: step(rest, s, True, CHUNK // 2),
                lambda s: step(rest, s, True, CHUNK),
                state,
            )
            out = jnp.concatenate([(accum / total).astype(jnp.bfloat16) for _, total, accum in state], axis=0)
            store(j, lambda h, b: out[h * PAGE + b * 32 : h * PAGE + b * 32 + 32, :])

        @pl.when(j >= live)
        def _():
            store(j, lambda h, b: jnp.zeros((32, HD), jnp.bfloat16))


def attend(counts, order, place, q, own, other):
    smem = pl.BlockSpec(memory_space=pltpu.SMEM)
    vmem = pl.BlockSpec(memory_space=pltpu.VMEM)
    return pl.pallas_call(
        attention_kernel,
        out_shape=jax.ShapeDtypeStruct((ZH, X, 32, HEADS * HD), jnp.bfloat16),
        in_specs=[smem, smem, smem, vmem, vmem, vmem],
        out_specs=vmem,
        scratch_shapes=[pltpu.VMEM((PAGES * PAGE, HD), jnp.bfloat16) for _ in range(2)],
        compiler_params=pltpu.CompilerParams(vmem_limit_bytes=40 << 20),
    )(counts, order, place, q, own, other)


def project_kernel(me, a_ref, b_ref, w_ref, o_ref):
    half = a_ref.shape[-1]
    w = jnp.concatenate([w_ref[0, 0], w_ref[0, 1]], axis=1)
    part = jnp.dot(a_ref[...].reshape(-1, half), w[:half], preferred_element_type=jnp.float32)
    part += jnp.dot(b_ref[...].reshape(-1, half), w[half:], preferred_element_type=jnp.float32)
    part = part.astype(jnp.bfloat16).reshape(QUAD, X, 32, 2 * HD)
    for i in range(QUAD):
        o_ref[:, me[0] ^ i] = part[i]


def project(me, a, b, w):
    rows = pl.BlockSpec(a.shape, lambda i: (0, 0, 0, 0))
    return pl.pallas_call(
        project_kernel,
        grid=(Y,),
        out_shape=jax.ShapeDtypeStruct((X, QUAD, 32, ZL * HD), jnp.bfloat16),
        in_specs=[pl.BlockSpec(memory_space=pltpu.SMEM), rows, rows, pl.BlockSpec((1, *w.shape[1:]), lambda i: (i, 0, 0, 0))],
        out_specs=pl.BlockSpec((X, QUAD, 32, 2 * HD), lambda i: (0, 0, 0, i)),
        compiler_params=pltpu.CompilerParams(vmem_limit_bytes=24 << 20),
    )(me, a, b, w)


def spread(piece, axis, count):
    return lax.all_to_all(jnp.broadcast_to(piece[None], (count, *piece.shape)), axis, 0, 0)


def swap(piece, axis):
    return lax.ppermute(piece, axis, [(0, 1), (1, 0)])


def quad(piece, step):
    return lax.ppermute(piece, ("zb", "zq"), [(i, i ^ step) for i in range(QUAD)])


def around(piece, axis, count, shift):
    return lax.ppermute(piece, axis, [((i + shift) % count, i) for i in range(count)])


def along(piece, step):
    def place(z, c):
        return ((z % ZL) * ZH + z // ZL) * C + c

    perm = [(place(z, c), place((z + step(z, c)) % Z, c)) for z in range(Z) for c in range(C)]
    return lax.ppermute(piece, LINE, perm)


def body(counts, order, queries, keys, values, weight):
    za, zb, zq, y, zh, x, c = (lax.axis_index(name) for name in ("za", "zb", "zq", "y", "zh", "x", "c"))
    zl = (za * ZB + zb) * ZQ + zq

    def piece(step):
        owner = (zh * ZL + zl + step + Z) % Z // ZL
        head = (owner * X + x) * HD
        return jnp.where(
            c == 0,
            lax.dynamic_slice_in_dim(keys, head, HD, 1),
            lax.dynamic_slice_in_dim(values, head, HD, 1),
        )

    with jax.named_scope("cache_gather"):
        near = [
            piece(0),
            along(piece(-2), lambda z, c: -2),
            along(piece(8 * c - 4), lambda z, c: 8 * c - 4),
            along(piece(2), lambda z, c: 2),
        ]
        near, weight = lax.optimization_barrier((near, weight))
        near = jnp.concatenate(near, axis=0)
        near = jnp.concatenate([near, swap(near, "zq")], axis=0)
    with jax.named_scope("weight_gather"):
        given = swap(lax.dynamic_slice_in_dim(weight, (1 - c) * HD, HD, 1), "c")
        kept = lax.dynamic_slice_in_dim(weight, c * HD, HD, 1)
        narrow = jnp.concatenate([kept, given], axis=0)
        near, narrow = lax.optimization_barrier((near, narrow))
        facing = swap(narrow, "za")
    with jax.named_scope("cache_gather"):
        own = spread(near, "y", Y).reshape(N_SEQ * ROWS, HD)
        own, narrow, facing = lax.optimization_barrier((own, narrow, facing))
        other = swap(own, "c")
    with jax.named_scope("weight_gather"):
        wide = jnp.stack([jnp.where(za == 0, narrow, facing), jnp.where(za == 0, facing, narrow)])
        wide = spread(wide, "y", Y)
    with jax.named_scope("attention"):
        place = jnp.stack([zl * Y + y, c, zh]).astype(jnp.int32)
        heads = attend(counts, order, place, queries, own, other)

    def projected(mine):
        with jax.named_scope("rows_gather"):
            theirs = swap(mine, "c")
        with jax.named_scope("projection"):
            here = jnp.reshape(zb * ZQ + zq, (1,)).astype(jnp.int32)
            return project(here, mine, theirs, wide)

    def part_of(parts, shift):
        return lax.dynamic_index_in_dim(parts, (x + shift) % X, 0, keepdims=False)

    with jax.named_scope("rows_gather"):
        first, second = (jnp.stack([rows] + [quad(rows, step) for step in range(1, QUAD)]) for rows in heads)
        first, wide = lax.optimization_barrier((first, wide))
    parts = projected(first)
    with jax.named_scope("sum_x"):
        away = lax.all_to_all(parts, "x", 0, 0)
        away = jnp.sum(away.astype(jnp.float32), axis=0).astype(jnp.bfloat16)
        away, second = lax.optimization_barrier((away, second))
    with jax.named_scope("sum_zh"):
        back = spread(away, "zh", ZH)
        back = lax.dynamic_index_in_dim(back, 1 - zh, 0, keepdims=False)
    parts = projected(second)
    with jax.named_scope("sum_x"):
        stay = part_of(parts, 0).astype(jnp.float32)
        for shift in range(1, X):
            stay += around(part_of(parts, X - shift), "x", X, shift).astype(jnp.float32)
    with jax.named_scope("columns"):
        mixed = (stay + back.astype(jnp.float32)).astype(jnp.bfloat16)
        mixed = lax.all_to_all(mixed.reshape(QUAD * C, 16, ZL * HD), ("zb", "zq", "c"), 0, 0)
        mixed = mixed.reshape(ZB, ZQ, C, 16, Y, ZA, HD).transpose(3, 5, 0, 1, 4, 2, 6)
    return mixed.reshape(16, N_SEQ * 256)


def solution(mesh):
    fine = Mesh(mesh.devices.reshape(ZA, ZB, ZQ, Y, ZH, X, C), ("za", "zb", "zq", "y", "zh", "x", "c"))
    seq, tp = ("za", "zb", "zq", "y"), ("zh", "x", "c")
    return jax.shard_map(
        body,
        mesh=fine,
        in_specs=(P(), P(), P(seq, tp), P(seq, None), P(seq, None), P(tp, seq)),
        out_specs=P((*seq, *tp), None),
        check_vma=False,
    )
```

```python
import math

import jax
import jax.numpy as jnp
from jax import lax
from jax.experimental import pallas as pl
from jax.experimental.pallas import tpu as pltpu
from jax.sharding import Mesh, PartitionSpec as P

HD = 128
PAGE = 64
SLOTS = 4
PAGES = 64
HEADS = 4
ZA, ZB, ZQ, Y, ZH, X, C = 2, 2, 2, 4, 2, 4, 2
ZL, QUAD = ZA * ZB * ZQ, ZB * ZQ
Z = ZH * ZL
LINE = ("za", "zb", "zq", "zh", "c")
N_SEQ = ZL * Y
ROWS = SLOTS * PAGE
CHUNK = 2048
SCALE = HD**-0.5 * math.log2(math.e)


def attention_kernel(counts, order, place, q_ref, own_ref, other_ref, o_ref, k_sc, v_sc):
    me = place[0]
    core = place[1]
    my_zh = place[2]
    my_z = me // Y

    def sort_pages(k_ref, v_ref):
        def one(rank, at):
            d, j = at
            z = d // Y
            far = (z + my_z) % 2
            near = my_z + far * (1 - 2 * (my_z % 2))
            base = (d % Y) * ZL + far * (ZL // 2) + (z - near + ZL) % ZL // 2
            src = pl.multiple_of(base * ROWS + j * PAGE, PAGE)
            to = pl.multiple_of(order[rank] * PAGE, PAGE)
            k_sc[pl.ds(to, PAGE), :] = k_ref[pl.ds(src, PAGE), :]
            v_sc[pl.ds(to, PAGE), :] = v_ref[pl.ds(src, PAGE), :]
            last = j + 1 >= counts[d]
            return jnp.where(last, jnp.minimum(d + 1, N_SEQ - 1), d), jnp.where(last, 0, j + 1)

        lax.fori_loop(0, PAGES, one, (jnp.int32(0), jnp.int32(0)), unroll=4)

    @pl.when(core == 0)
    def _():
        sort_pages(own_ref, other_ref)

    @pl.when(core == 1)
    def _():
        sort_pages(other_ref, own_ref)

    before = lax.fori_loop(0, me, lambda d, s: s + counts[d], jnp.int32(0))
    live = counts[me]

    def store(j, rows):
        kept = (my_zh == j // 2).astype(jnp.int32)
        for b in range(2):
            for h in range(HEADS):
                o_ref[kept, 2 * (j % 2) + b, :, h * HD : (h + 1) * HD] = rows(h, b)

    for j in range(SLOTS):

        @pl.when(j < live)
        def _():
            page = order[before + j]
            groups = 1
            count = HEADS // groups
            q = [
                jnp.concatenate(
                    [q_ref[j * PAGE : (j + 1) * PAGE, h * HD : (h + 1) * HD] for h in range(g * count, (g + 1) * count)],
                    axis=0,
                )
                for g in range(groups)
            ]
            size = count * PAGE

            def step(at, state, last, CHUNK):
                k = k_sc[pl.ds(at, CHUNK), :]
                v = v_sc[pl.ds(at, CHUNK), :]
                if last:
                    row = lax.broadcasted_iota(jnp.int32, (size, CHUNK), 0) % PAGE + page * PAGE
                    seen = lax.broadcasted_iota(jnp.int32, (size, CHUNK), 1) + at <= row
                out = []
                for g in range(groups):
                    best, total, accum = state[g]
                    s = lax.dot_general(q[g], k, (((1,), (1,)), ((), ())), preferred_element_type=jnp.float32)
                    if last:
                        s = jnp.where(seen, s, jnp.float32(-1e30))
                    new = jnp.maximum(best, jnp.max(s, axis=1, keepdims=True))
                    p = jnp.exp2((s - new) * SCALE)
                    fade = jnp.exp2((best - new) * SCALE)
                    total = total * fade + jnp.sum(p, axis=1, keepdims=True)
                    accum = accum * fade + jnp.dot(p.astype(jnp.bfloat16), v, preferred_element_type=jnp.float32)
                    out.append((new, total, accum))
                return tuple(out)

            state = tuple(
                (
                    jnp.full((size, 1), -1e30, jnp.float32),
                    jnp.zeros((size, 1), jnp.float32),
                    jnp.zeros((size, HD), jnp.float32),
                )
                for _ in range(groups)
            )
            full = page // (CHUNK // PAGE)
            state = lax.fori_loop(
                0, full, lambda i, s: step(pl.multiple_of(i * CHUNK, CHUNK), s, False, CHUNK), state
            )
            rest = pl.multiple_of(full * CHUNK, CHUNK)
            state = lax.cond(
                page % (CHUNK // PAGE) < CHUNK // PAGE // 2,
                lambda s: step(rest, s, True, CHUNK // 2),
                lambda s: step(rest, s, True, CHUNK),
                state,
            )
            out = jnp.concatenate([(accum / total).astype(jnp.bfloat16) for _, total, accum in state], axis=0)
            store(j, lambda h, b: out[h * PAGE + b * 32 : h * PAGE + b * 32 + 32, :])

        @pl.when(j >= live)
        def _():
            store(j, lambda h, b: jnp.zeros((32, HD), jnp.bfloat16))


def attend(counts, order, place, q, own, other):
    smem = pl.BlockSpec(memory_space=pltpu.SMEM)
    vmem = pl.BlockSpec(memory_space=pltpu.VMEM)
    return pl.pallas_call(
        attention_kernel,
        out_shape=jax.ShapeDtypeStruct((ZH, X, 32, HEADS * HD), jnp.bfloat16),
        in_specs=[smem, smem, smem, vmem, vmem, vmem],
        out_specs=vmem,
        scratch_shapes=[pltpu.VMEM((PAGES * PAGE, HD), jnp.bfloat16) for _ in range(2)],
        compiler_params=pltpu.CompilerParams(vmem_limit_bytes=40 << 20),
    )(counts, order, place, q, own, other)


def project_kernel(me, a_ref, b_ref, w_ref, o_ref):
    half = a_ref.shape[-1]
    w = jnp.concatenate([w_ref[0, 0], w_ref[0, 1]], axis=1)
    part = jnp.dot(a_ref[...].reshape(-1, half), w[:half], preferred_element_type=jnp.float32)
    part += jnp.dot(b_ref[...].reshape(-1, half), w[half:], preferred_element_type=jnp.float32)
    part = part.astype(jnp.bfloat16).reshape(QUAD, X, 32, 2 * HD)
    for i in range(QUAD):
        o_ref[:, me[0] ^ ((QUAD - i) % QUAD)] = part[i]


def project(me, a, b, w):
    rows = pl.BlockSpec(a.shape, lambda i: (0, 0, 0, 0))
    return pl.pallas_call(
        project_kernel,
        grid=(Y,),
        out_shape=jax.ShapeDtypeStruct((X, QUAD, 32, ZL * HD), jnp.bfloat16),
        in_specs=[pl.BlockSpec(memory_space=pltpu.SMEM), rows, rows, pl.BlockSpec((1, *w.shape[1:]), lambda i: (i, 0, 0, 0))],
        out_specs=pl.BlockSpec((X, QUAD, 32, 2 * HD), lambda i: (0, 0, 0, i)),
        compiler_params=pltpu.CompilerParams(vmem_limit_bytes=24 << 20),
    )(me, a, b, w)


def spread(piece, axis, count):
    return lax.all_to_all(jnp.broadcast_to(piece[None], (count, *piece.shape)), axis, 0, 0)


def swap(piece, axis):
    return lax.ppermute(piece, axis, [(0, 1), (1, 0)])


def quad(piece, step):
    return lax.ppermute(piece, ("zb", "zq"), [(i, i ^ step) for i in range(QUAD)])


def around(piece, axis, count, shift):
    return lax.ppermute(piece, axis, [((i + shift) % count, i) for i in range(count)])


def along(piece, step):
    def place(z, c):
        return ((z % ZL) * ZH + z // ZL) * C + c

    perm = [(place(z, c), place((z + step(z, c)) % Z, c)) for z in range(Z) for c in range(C)]
    return lax.ppermute(piece, LINE, perm)


def body(counts, order, queries, keys, values, weight):
    za, zb, zq, y, zh, x, c = (lax.axis_index(name) for name in ("za", "zb", "zq", "y", "zh", "x", "c"))
    zl = (za * ZB + zb) * ZQ + zq

    def piece(step):
        owner = (zh * ZL + zl + step + Z) % Z // ZL
        head = (owner * X + x) * HD
        return jnp.where(
            c == 0,
            lax.dynamic_slice_in_dim(keys, head, HD, 1),
            lax.dynamic_slice_in_dim(values, head, HD, 1),
        )

    with jax.named_scope("cache_gather"):
        here = piece(0)
        up = along(piece(-2), lambda z, c: -2)
        down = along(piece(2), lambda z, c: 2)
        far = along(piece(8 * c - 4), lambda z, c: 8 * c - 4)
        side = along(piece(jnp.where(zq == 1, 3, -3)), lambda z, c: 3 if z % 2 else -3)
        near = jnp.concatenate([here, up, down], axis=0)
        near, weight = lax.optimization_barrier((near, weight))
        beside = swap(near, "zq")
        near = jnp.concatenate(
            [near[: 2 * ROWS], far, near[2 * ROWS :], beside[: 2 * ROWS], side, beside[2 * ROWS :]], axis=0
        )
    with jax.named_scope("weight_gather"):
        given = swap(lax.dynamic_slice_in_dim(weight, (1 - c) * HD, HD, 1), "c")
        kept = lax.dynamic_slice_in_dim(weight, c * HD, HD, 1)
        narrow = jnp.concatenate([kept, given], axis=0)
        near, narrow = lax.optimization_barrier((near, narrow))
        facing = swap(narrow, "za")
    with jax.named_scope("cache_gather"):
        own = spread(near, "y", Y).reshape(N_SEQ * ROWS, HD)
        own, narrow, facing = lax.optimization_barrier((own, narrow, facing))
        other = swap(own, "c")
    with jax.named_scope("weight_gather"):
        wide = jnp.stack([jnp.where(za == 0, narrow, facing), jnp.where(za == 0, facing, narrow)])
        wide = spread(wide, "y", Y)
    with jax.named_scope("attention"):
        place = jnp.stack([zl * Y + y, c, zh]).astype(jnp.int32)
        heads = attend(counts, order, place, queries, own, other)

    def projected(mine, theirs):
        with jax.named_scope("projection"):
            here = jnp.reshape(zb * ZQ + zq, (1,)).astype(jnp.int32)
            return project(here, mine, theirs, wide)

    def part_of(parts, shift):
        return lax.dynamic_index_in_dim(parts, (x + shift) % X, 0, keepdims=False)

    with jax.named_scope("rows_gather"):
        first, second = (
            jnp.stack([rows] + [quad(rows, step) for step in range(QUAD - 1, 0, -1)]) for rows in heads
        )
        theirs = swap(first, "c")
        first, theirs, wide = lax.optimization_barrier((first, theirs, wide))
    parts = projected(first, theirs)
    with jax.named_scope("sum_x"):
        away = lax.all_to_all(parts, "x", 0, 0)
        away = jnp.sum(away.astype(jnp.float32), axis=0).astype(jnp.bfloat16)
        away = jnp.broadcast_to(away[None], (ZH, *away.shape))
        away, second = lax.optimization_barrier((away, second))
        theirs = swap(second, "c")
    with jax.named_scope("sum_zh"):
        back = lax.all_to_all(away, "zh", 0, 0)
        back = lax.dynamic_index_in_dim(back, 1 - zh, 0, keepdims=False)
    parts = projected(second, theirs)
    with jax.named_scope("sum_x"):
        stay = part_of(parts, 0).astype(jnp.float32)
        for shift in range(X - 1, 0, -1):
            stay += around(part_of(parts, X - shift), "x", X, shift).astype(jnp.float32)
    with jax.named_scope("columns"):
        mixed = (stay + back.astype(jnp.float32)).astype(jnp.bfloat16)
        mixed = lax.all_to_all(mixed.reshape(QUAD * C, 16, ZL * HD), ("zb", "zq", "c"), 0, 0)
        mixed = mixed.reshape(ZB, ZQ, C, 16, Y, ZA, HD).transpose(3, 5, 0, 1, 4, 2, 6)
    return mixed.reshape(16, N_SEQ * 256)


def solution(mesh):
    fine = Mesh(mesh.devices.reshape(ZA, ZB, ZQ, Y, ZH, X, C), ("za", "zb", "zq", "y", "zh", "x", "c"))
    seq, tp = ("za", "zb", "zq", "y"), ("zh", "x", "c")
    return jax.shard_map(
        body,
        mesh=fine,
        in_specs=(P(), P(), P(seq, tp), P(seq, None), P(seq, None), P(tp, seq)),
        out_specs=P((*seq, *tp), None),
        check_vma=False,
    )
```

```python
import math

import jax
import jax.numpy as jnp
from jax import lax
from jax.experimental import pallas as pl
from jax.experimental.pallas import tpu as pltpu
from jax.sharding import Mesh, PartitionSpec as P

HD = 128
PAGE = 64
SLOTS = 4
PAGES = 64
HEADS = 4
ZA, ZB, ZQ, Y, ZH, X, C = 2, 2, 2, 4, 2, 4, 2
ZL, QUAD = ZA * ZB * ZQ, ZB * ZQ
Z = ZH * ZL
LINE = ("za", "zb", "zq", "zh", "c")
N_SEQ = ZL * Y
ROWS = SLOTS * PAGE
CHUNK = 2048
SCALE = HD**-0.5 * math.log2(math.e)


def attention_kernel(counts, order, place, q_ref, own_ref, other_ref, o_ref, k_sc, v_sc):
    me = place[0]
    core = place[1]
    my_z = me // Y

    def sort_pages(k_ref, v_ref):
        def one(rank, at):
            d, j = at
            z = d // Y
            far = (z + my_z) % 2
            near = my_z + far * (1 - 2 * (my_z % 2))
            base = (d % Y) * ZL + far * (ZL // 2) + (z - near + ZL) % ZL // 2
            src = pl.multiple_of(base * ROWS + j * PAGE, PAGE)
            to = pl.multiple_of(order[rank] * PAGE, PAGE)
            k_sc[pl.ds(to, PAGE), :] = k_ref[pl.ds(src, PAGE), :]
            v_sc[pl.ds(to, PAGE), :] = v_ref[pl.ds(src, PAGE), :]
            last = j + 1 >= counts[d]
            return jnp.where(last, jnp.minimum(d + 1, N_SEQ - 1), d), jnp.where(last, 0, j + 1)

        lax.fori_loop(0, PAGES, one, (jnp.int32(0), jnp.int32(0)), unroll=4)

    before = lax.fori_loop(0, me, lambda d, s: s + counts[d], jnp.int32(0))
    live = counts[me]
    head = place[2] * 2

    @pl.when((head < live) & (core == 0))
    def _():
        sort_pages(own_ref, other_ref)

    @pl.when((head < live) & (core == 1))
    def _():
        sort_pages(other_ref, own_ref)

    def store(i, rows):
        for b in range(2):
            for h in range(HEADS):
                o_ref[2 * i + b, :, h * HD : (h + 1) * HD] = rows(h, b)

    for i in range(2):
        j = head + i
        here = pl.ds(pl.multiple_of(j * PAGE, PAGE), PAGE)

        @pl.when(j < live)
        def _():
            page = order[before + j]
            q = jnp.concatenate([q_ref[here, h * HD : (h + 1) * HD] for h in range(HEADS)], axis=0)
            size = HEADS * PAGE

            def step(at, state, masked, width):
                best, total, accum = state
                k = k_sc[pl.ds(at, width), :]
                v = v_sc[pl.ds(at, width), :]
                s = lax.dot_general(q, k, (((1,), (1,)), ((), ())), preferred_element_type=jnp.float32)
                if masked:
                    row = lax.broadcasted_iota(jnp.int32, s.shape, 0) % PAGE + page * PAGE
                    seen = lax.broadcasted_iota(jnp.int32, s.shape, 1) + at <= row
                    s = jnp.where(seen, s, jnp.float32(-1e30))
                new = jnp.maximum(best, jnp.max(s, axis=1, keepdims=True))
                p = jnp.exp2((s - new) * SCALE)
                fade = jnp.exp2((best - new) * SCALE)
                total = total * fade + jnp.sum(p, axis=1, keepdims=True)
                accum = accum * fade + jnp.dot(p.astype(jnp.bfloat16), v, preferred_element_type=jnp.float32)
                return new, total, accum

            state = (
                jnp.full((size, 1), -1e30, jnp.float32),
                jnp.zeros((size, 1), jnp.float32),
                jnp.zeros((size, HD), jnp.float32),
            )
            full = page // (CHUNK // PAGE)
            state = lax.fori_loop(
                0, full, lambda i, s: step(pl.multiple_of(i * CHUNK, CHUNK), s, False, CHUNK), state
            )
            rest = pl.multiple_of(full * CHUNK, CHUNK)
            state = lax.cond(
                page % (CHUNK // PAGE) < CHUNK // PAGE // 2,
                lambda s: step(rest, s, True, CHUNK // 2),
                lambda s: step(rest, s, True, CHUNK),
                state,
            )
            _, total, accum = state
            out = (accum / total).astype(jnp.bfloat16)
            store(i, lambda h, b: out[h * PAGE + b * 32 : h * PAGE + b * 32 + 32, :])

        @pl.when(j >= live)
        def _():
            store(i, lambda h, b: jnp.zeros((32, HD), jnp.bfloat16))


def attend(counts, order, place, q, own, other):
    smem = pl.BlockSpec(memory_space=pltpu.SMEM)
    vmem = pl.BlockSpec(memory_space=pltpu.VMEM)
    return pl.pallas_call(
        attention_kernel,
        out_shape=jax.ShapeDtypeStruct((X, 32, HEADS * HD), jnp.bfloat16),
        in_specs=[smem, smem, smem, vmem, vmem, vmem],
        out_specs=vmem,
        scratch_shapes=[pltpu.VMEM((PAGES * PAGE, HD), jnp.bfloat16) for _ in range(2)],
        compiler_params=pltpu.CompilerParams(vmem_limit_bytes=40 << 20),
    )(counts, order, place, q, own, other)


def project_kernel(me, a_ref, b_ref, w_ref, o_ref):
    half = a_ref.shape[-1]
    w = jnp.concatenate([w_ref[0, 0], w_ref[0, 1]], axis=1)
    part = jnp.dot(a_ref[...].reshape(-1, half), w[:half], preferred_element_type=jnp.float32)
    part += jnp.dot(b_ref[...].reshape(-1, half), w[half:], preferred_element_type=jnp.float32)
    part = part.astype(jnp.bfloat16).reshape(QUAD, X, 32, 2 * HD)
    for i in range(QUAD):
        o_ref[:, me[0] ^ ((QUAD - i) % QUAD)] = part[i]


def project(me, a, b, w):
    rows = pl.BlockSpec(a.shape, lambda i: (0, 0, 0, 0))
    return pl.pallas_call(
        project_kernel,
        grid=(Y,),
        out_shape=jax.ShapeDtypeStruct((X, QUAD, 32, ZL * HD), jnp.bfloat16),
        in_specs=[pl.BlockSpec(memory_space=pltpu.SMEM), rows, rows, pl.BlockSpec((1, *w.shape[1:]), lambda i: (i, 0, 0, 0))],
        out_specs=pl.BlockSpec((X, QUAD, 32, 2 * HD), lambda i: (0, 0, 0, i)),
        compiler_params=pltpu.CompilerParams(vmem_limit_bytes=24 << 20),
    )(me, a, b, w)


def add_kernel(p_ref, o_ref):
    total = p_ref[0].astype(jnp.float32)
    for i in range(1, X):
        total += p_ref[i].astype(jnp.float32)
    o_ref[0] = total.astype(jnp.bfloat16)
    o_ref[1] = total.astype(jnp.bfloat16)


def add_parts(parts):
    return pl.pallas_call(
        add_kernel,
        grid=(QUAD,),
        out_shape=jax.ShapeDtypeStruct((ZH, *parts.shape[1:]), jnp.bfloat16),
        in_specs=[pl.BlockSpec((X, 1, *parts.shape[2:]), lambda i: (0, i, 0, 0))],
        out_specs=pl.BlockSpec((ZH, 1, *parts.shape[2:]), lambda i: (0, i, 0, 0)),
        compiler_params=pltpu.CompilerParams(vmem_limit_bytes=16 << 20),
    )(parts)


def spread(piece, axis, count):
    return lax.all_to_all(jnp.broadcast_to(piece[None], (count, *piece.shape)), axis, 0, 0)


def swap(piece, axis):
    return lax.ppermute(piece, axis, [(0, 1), (1, 0)])


def quad(piece, step):
    return lax.ppermute(piece, ("zb", "zq"), [(i, i ^ step) for i in range(QUAD)])


def around(piece, axis, count, shift):
    return lax.ppermute(piece, axis, [((i + shift) % count, i) for i in range(count)])


def along(piece, step):
    def place(z, c):
        return ((z % ZL) * ZH + z // ZL) * C + c

    perm = [(place(z, c), place((z + step(z, c)) % Z, c)) for z in range(Z) for c in range(C)]
    return lax.ppermute(piece, LINE, perm)


def body(counts, order, queries, keys, values, weight):
    za, zb, zq, y, zh, x, c = (lax.axis_index(name) for name in ("za", "zb", "zq", "y", "zh", "x", "c"))
    zl = (za * ZB + zb) * ZQ + zq

    def piece(step):
        owner = (zh * ZL + zl + step + Z) % Z // ZL
        head = (owner * X + x) * HD
        return jnp.where(
            c == 0,
            lax.dynamic_slice_in_dim(keys, head, HD, 1),
            lax.dynamic_slice_in_dim(values, head, HD, 1),
        )

    with jax.named_scope("cache_gather"):
        here = piece(0)
        up = along(piece(-2), lambda z, c: -2)
        down = along(piece(2), lambda z, c: 2)
        far = along(piece(8 * c - 4), lambda z, c: 8 * c - 4)
        side = along(piece(jnp.where(zq == 1, 3, -3)), lambda z, c: 3 if z % 2 else -3)
        near = jnp.concatenate([here, up, down], axis=0)
        near, weight = lax.optimization_barrier((near, weight))
        beside = swap(near, "zq")
        near = jnp.concatenate(
            [near[: 2 * ROWS], far, near[2 * ROWS :], beside[: 2 * ROWS], side, beside[2 * ROWS :]], axis=0
        )
    with jax.named_scope("weight_gather"):
        given = swap(lax.dynamic_slice_in_dim(weight, (1 - c) * HD, HD, 1), "c")
        kept = lax.dynamic_slice_in_dim(weight, c * HD, HD, 1)
        narrow = jnp.concatenate([kept, given], axis=0)
        near, narrow = lax.optimization_barrier((near, narrow))
        facing = swap(narrow, "za")
    with jax.named_scope("cache_gather"):
        own = spread(near, "y", Y).reshape(N_SEQ * ROWS, HD)
        own, narrow, facing = lax.optimization_barrier((own, narrow, facing))
        other = swap(own, "c")
    with jax.named_scope("weight_gather"):
        wide = jnp.stack([jnp.where(za == 0, narrow, facing), jnp.where(za == 0, facing, narrow)])
        wide = spread(wide, "y", Y)
    with jax.named_scope("attention"):
        heads = [
            attend(counts, order, jnp.stack([zl * Y + y, c, half]).astype(jnp.int32), queries, own, other)
            for half in (1 - zh, zh)
        ]

    def projected(mine, theirs):
        with jax.named_scope("projection"):
            here = jnp.reshape(zb * ZQ + zq, (1,)).astype(jnp.int32)
            return project(here, mine, theirs, wide)

    def part_of(parts, shift):
        return lax.dynamic_index_in_dim(parts, (x + shift) % X, 0, keepdims=False)

    def gather_rows(rows):
        return jnp.stack([rows] + [quad(rows, step) for step in range(QUAD - 1, 0, -1)])

    with jax.named_scope("rows_gather"):
        first = gather_rows(heads[0])
        first, later = lax.optimization_barrier((first, heads[1]))
        theirs = swap(first, "c")
        first, theirs, wide = lax.optimization_barrier((first, theirs, wide))
        second = gather_rows(later)
    parts = projected(first, theirs)
    with jax.named_scope("sum_x"):
        away = add_parts(lax.all_to_all(parts, "x", 0, 0))
        away, second = lax.optimization_barrier((away, second))
        theirs = swap(second, "c")
    with jax.named_scope("sum_zh"):
        back = lax.all_to_all(away, "zh", 0, 0)
        back = lax.dynamic_index_in_dim(back, 1 - zh, 0, keepdims=False)
    parts = projected(second, theirs)
    with jax.named_scope("sum_x"):
        stay = part_of(parts, 0).astype(jnp.float32)
        for shift in range(X - 1, 0, -1):
            stay += around(part_of(parts, X - shift), "x", X, shift).astype(jnp.float32)
    with jax.named_scope("columns"):
        mixed = (stay + back.astype(jnp.float32)).astype(jnp.bfloat16)
        mixed = lax.all_to_all(mixed.reshape(QUAD * C, 16, ZL * HD), ("zb", "zq", "c"), 0, 0)
        mixed = mixed.reshape(ZB, ZQ, C, 16, Y, ZA, HD).transpose(3, 5, 0, 1, 4, 2, 6)
    return mixed.reshape(16, N_SEQ * 256)


def solution(mesh):
    fine = Mesh(mesh.devices.reshape(ZA, ZB, ZQ, Y, ZH, X, C), ("za", "zb", "zq", "y", "zh", "x", "c"))
    seq, tp = ("za", "zb", "zq", "y"), ("zh", "x", "c")
    return jax.shard_map(
        body,
        mesh=fine,
        in_specs=(P(), P(), P(seq, tp), P(seq, None), P(seq, None), P(tp, seq)),
        out_specs=P((*seq, *tp), None),
        check_vma=False,
    )
```

```python
import math

import jax
import jax.numpy as jnp
from jax import lax
from jax.experimental import pallas as pl
from jax.experimental.pallas import tpu as pltpu
from jax.sharding import Mesh, PartitionSpec as P

HD = 128
PAGE = 64
SLOTS = 4
PAGES = 64
HEADS = 4
ZA, ZB, ZQ, Y, ZH, X, C = 2, 2, 2, 4, 2, 4, 2
ZL, QUAD = ZA * ZB * ZQ, ZB * ZQ
Z = ZH * ZL
LINE = ("za", "zb", "zq", "zh", "c")
N_SEQ = ZL * Y
ROWS = SLOTS * PAGE
CHUNK = 2048
SCALE = HD**-0.5 * math.log2(math.e)


def attention_kernel(counts, order, place, q_ref, own_ref, other_ref, o_ref, k_sc, v_sc):
    me = place[0]
    core = place[1]
    my_z = me // Y

    def sort_pages(k_ref, v_ref):
        def one(rank, at):
            d, j = at
            z = d // Y
            far = (z + my_z) % 2
            near = my_z + far * (1 - 2 * (my_z % 2))
            base = (d % Y) * ZL + far * (ZL // 2) + (z - near + ZL) % ZL // 2
            src = pl.multiple_of(base * ROWS + j * PAGE, PAGE)
            to = pl.multiple_of(order[rank] * PAGE, PAGE)
            k_sc[pl.ds(to, PAGE), :] = k_ref[pl.ds(src, PAGE), :]
            v_sc[pl.ds(to, PAGE), :] = v_ref[pl.ds(src, PAGE), :]
            last = j + 1 >= counts[d]
            return jnp.where(last, jnp.minimum(d + 1, N_SEQ - 1), d), jnp.where(last, 0, j + 1)

        lax.fori_loop(0, PAGES, one, (jnp.int32(0), jnp.int32(0)), unroll=4)

    before = lax.fori_loop(0, me, lambda d, s: s + counts[d], jnp.int32(0))
    live = counts[me]
    head = place[2] * 2

    @pl.when((head < live) & (core == 0))
    def _():
        sort_pages(own_ref, other_ref)

    @pl.when((head < live) & (core == 1))
    def _():
        sort_pages(other_ref, own_ref)

    def store(i, rows):
        for b in range(2):
            for h in range(HEADS):
                o_ref[2 * i + b, :, h * HD : (h + 1) * HD] = rows(h, b)

    for i in range(2):
        j = head + i
        here = pl.ds(pl.multiple_of(j * PAGE, PAGE), PAGE)

        @pl.when(j < live)
        def _():
            page = order[before + j]
            q = jnp.concatenate([q_ref[here, h * HD : (h + 1) * HD] for h in range(HEADS)], axis=0)
            size = HEADS * PAGE

            def step(at, state, masked, width):
                best, total, accum = state
                k = k_sc[pl.ds(at, width), :]
                v = v_sc[pl.ds(at, width), :]
                s = lax.dot_general(q, k, (((1,), (1,)), ((), ())), preferred_element_type=jnp.float32)
                if masked:
                    row = lax.broadcasted_iota(jnp.int32, s.shape, 0) % PAGE + page * PAGE
                    seen = lax.broadcasted_iota(jnp.int32, s.shape, 1) + at <= row
                    s = jnp.where(seen, s, jnp.float32(-1e30))
                new = jnp.maximum(best, jnp.max(s, axis=1, keepdims=True))
                p = jnp.exp2((s - new) * SCALE)
                fade = jnp.exp2((best - new) * SCALE)
                total = total * fade + jnp.sum(p, axis=1, keepdims=True)
                accum = accum * fade + jnp.dot(p.astype(jnp.bfloat16), v, preferred_element_type=jnp.float32)
                return new, total, accum

            state = (
                jnp.full((size, 1), -1e30, jnp.float32),
                jnp.zeros((size, 1), jnp.float32),
                jnp.zeros((size, HD), jnp.float32),
            )
            full = page // (CHUNK // PAGE)
            state = lax.fori_loop(
                0, full, lambda i, s: step(pl.multiple_of(i * CHUNK, CHUNK), s, False, CHUNK), state
            )
            rest = pl.multiple_of(full * CHUNK, CHUNK)
            state = lax.cond(
                page % (CHUNK // PAGE) < CHUNK // PAGE // 2,
                lambda s: step(rest, s, True, CHUNK // 2),
                lambda s: step(rest, s, True, CHUNK),
                state,
            )
            _, total, accum = state
            out = (accum / total).astype(jnp.bfloat16)
            store(i, lambda h, b: out[h * PAGE + b * 32 : h * PAGE + b * 32 + 32, :])

        @pl.when(j >= live)
        def _():
            store(i, lambda h, b: jnp.zeros((32, HD), jnp.bfloat16))


def attend(counts, order, place, q, own, other):
    smem = pl.BlockSpec(memory_space=pltpu.SMEM)
    vmem = pl.BlockSpec(memory_space=pltpu.VMEM)
    return pl.pallas_call(
        attention_kernel,
        out_shape=jax.ShapeDtypeStruct((X, 32, HEADS * HD), jnp.bfloat16),
        in_specs=[smem, smem, smem, vmem, vmem, vmem],
        out_specs=vmem,
        scratch_shapes=[pltpu.VMEM((PAGES * PAGE, HD), jnp.bfloat16) for _ in range(2)],
        compiler_params=pltpu.CompilerParams(vmem_limit_bytes=40 << 20),
    )(counts, order, place, q, own, other)


def project_kernel(me, a_ref, b_ref, w_ref, o_ref):
    half = a_ref.shape[-1]
    w = jnp.concatenate([w_ref[i, j] for i in range(2) for j in range(ZA)], axis=1)
    rows = jnp.concatenate([a_ref[...].reshape(-1, half), b_ref[...].reshape(-1, half)], axis=1)
    part = jnp.dot(rows, w, preferred_element_type=jnp.float32)
    part = part.astype(jnp.bfloat16).reshape(QUAD, X, 32, 4 * HD)
    for i in range(QUAD):
        o_ref[:, me[0] ^ ((QUAD - i) % QUAD)] = part[i]


def project(me, a, b, w):
    rows = pl.BlockSpec(a.shape, lambda i: (0, 0, 0, 0))
    return pl.pallas_call(
        project_kernel,
        grid=(Y // 2,),
        out_shape=jax.ShapeDtypeStruct((X, QUAD, 32, ZL * HD), jnp.bfloat16),
        in_specs=[pl.BlockSpec(memory_space=pltpu.SMEM), rows, rows, pl.BlockSpec((2, *w.shape[1:]), lambda i: (i, 0, 0, 0))],
        out_specs=pl.BlockSpec((X, QUAD, 32, 4 * HD), lambda i: (0, 0, 0, i)),
        compiler_params=pltpu.CompilerParams(vmem_limit_bytes=24 << 20),
    )(me, a, b, w)


def add_kernel(p_ref, o_ref):
    total = p_ref[0].astype(jnp.float32)
    for i in range(1, X):
        total += p_ref[i].astype(jnp.float32)
    o_ref[0] = total.astype(jnp.bfloat16)
    o_ref[1] = total.astype(jnp.bfloat16)


def add_parts(parts):
    return pl.pallas_call(
        add_kernel,
        grid=(QUAD,),
        out_shape=jax.ShapeDtypeStruct((ZH, *parts.shape[1:]), jnp.bfloat16),
        in_specs=[pl.BlockSpec((X, 1, *parts.shape[2:]), lambda i: (0, i, 0, 0))],
        out_specs=pl.BlockSpec((ZH, 1, *parts.shape[2:]), lambda i: (0, i, 0, 0)),
        compiler_params=pltpu.CompilerParams(vmem_limit_bytes=16 << 20),
    )(parts)


def spread(piece, axis, count):
    return lax.all_to_all(jnp.broadcast_to(piece[None], (count, *piece.shape)), axis, 0, 0)


def swap(piece, axis):
    return lax.ppermute(piece, axis, [(0, 1), (1, 0)])


def quad(piece, step):
    return lax.ppermute(piece, ("zb", "zq"), [(i, i ^ step) for i in range(QUAD)])


def around(piece, axis, count, shift):
    return lax.ppermute(piece, axis, [((i + shift) % count, i) for i in range(count)])


def along(piece, step):
    def place(z, c):
        return ((z % ZL) * ZH + z // ZL) * C + c

    perm = [(place(z, c), place((z + step(z, c)) % Z, c)) for z in range(Z) for c in range(C)]
    return lax.ppermute(piece, LINE, perm)


def body(counts, order, queries, keys, values, weight):
    za, zb, zq, y, zh, x, c = (lax.axis_index(name) for name in ("za", "zb", "zq", "y", "zh", "x", "c"))
    zl = (za * ZB + zb) * ZQ + zq

    def piece(step):
        owner = (zh * ZL + zl + step + Z) % Z // ZL
        head = (owner * X + x) * HD
        return jnp.where(
            c == 0,
            lax.dynamic_slice_in_dim(keys, head, HD, 1),
            lax.dynamic_slice_in_dim(values, head, HD, 1),
        )

    with jax.named_scope("cache_gather"):
        here = piece(0)
        up = along(piece(-2), lambda z, c: -2)
        down = along(piece(2), lambda z, c: 2)
        far = along(piece(8 * c - 4), lambda z, c: 8 * c - 4)
        side = along(piece(jnp.where(zq == 1, 3, -3)), lambda z, c: 3 if z % 2 else -3)
        near = jnp.concatenate([here, up, down], axis=0)
        near, weight = lax.optimization_barrier((near, weight))
        beside = swap(near, "zq")
        near = jnp.concatenate(
            [near[: 2 * ROWS], far, near[2 * ROWS :], beside[: 2 * ROWS], side, beside[2 * ROWS :]], axis=0
        )
    with jax.named_scope("weight_gather"):
        given = swap(lax.dynamic_slice_in_dim(weight, (1 - c) * HD, HD, 1), "c")
        kept = lax.dynamic_slice_in_dim(weight, c * HD, HD, 1)
        narrow = jnp.concatenate([kept, given], axis=0)
        near, narrow = lax.optimization_barrier((near, narrow))
        facing = swap(narrow, "za")
    with jax.named_scope("cache_gather"):
        own = spread(near, "y", Y).reshape(N_SEQ * ROWS, HD)
        own, narrow, facing = lax.optimization_barrier((own, narrow, facing))
        other = swap(own, "c")
    with jax.named_scope("weight_gather"):
        wide = jnp.stack([jnp.where(za == 0, narrow, facing), jnp.where(za == 0, facing, narrow)])
        wide = spread(wide, "y", Y)
    with jax.named_scope("attention"):
        heads = [
            attend(counts, order, jnp.stack([zl * Y + y, c, half]).astype(jnp.int32), queries, own, other)
            for half in (1 - zh, zh)
        ]

    def projected(mine, theirs):
        with jax.named_scope("projection"):
            here = jnp.reshape(zb * ZQ + zq, (1,)).astype(jnp.int32)
            return project(here, mine, theirs, wide)

    def part_of(parts, shift):
        return lax.dynamic_index_in_dim(parts, (x + shift) % X, 0, keepdims=False)

    def gather_rows(rows):
        return jnp.stack([rows] + [quad(rows, step) for step in range(QUAD - 1, 0, -1)])

    with jax.named_scope("rows_gather"):
        first = gather_rows(heads[0])
        first, later = lax.optimization_barrier((first, heads[1]))
        theirs = swap(first, "c")
        first, theirs, wide = lax.optimization_barrier((first, theirs, wide))
        second = gather_rows(later)
    parts = projected(first, theirs)
    with jax.named_scope("sum_x"):
        away = add_parts(lax.all_to_all(parts, "x", 0, 0))
        away, second = lax.optimization_barrier((away, second))
        theirs = swap(second, "c")
    with jax.named_scope("sum_zh"):
        back = lax.all_to_all(away, "zh", 0, 0)
        back = lax.dynamic_index_in_dim(back, 1 - zh, 0, keepdims=False)
    parts = projected(second, theirs)
    with jax.named_scope("sum_x"):
        stay = part_of(parts, 0).astype(jnp.float32)
        for shift in range(X - 1, 0, -1):
            stay += around(part_of(parts, X - shift), "x", X, shift).astype(jnp.float32)
    with jax.named_scope("columns"):
        mixed = (stay + back.astype(jnp.float32)).astype(jnp.bfloat16)
        mixed = lax.all_to_all(mixed.reshape(QUAD * C, 16, ZL * HD), ("zb", "zq", "c"), 0, 0)
        mixed = mixed.reshape(ZB, ZQ, C, 16, Y, ZA, HD).transpose(3, 5, 0, 1, 4, 2, 6)
    return mixed.reshape(16, N_SEQ * 256)


def solution(mesh):
    fine = Mesh(mesh.devices.reshape(ZA, ZB, ZQ, Y, ZH, X, C), ("za", "zb", "zq", "y", "zh", "x", "c"))
    seq, tp = ("za", "zb", "zq", "y"), ("zh", "x", "c")
    return jax.shard_map(
        body,
        mesh=fine,
        in_specs=(P(), P(), P(seq, tp), P(seq, None), P(seq, None), P(tp, seq)),
        out_specs=P((*seq, *tp), None),
        check_vma=False,
    )
```

```python
import math

import jax
import jax.numpy as jnp
from jax import lax
from jax.experimental import pallas as pl
from jax.experimental.pallas import tpu as pltpu
from jax.sharding import Mesh, PartitionSpec as P

HD = 128
PAGE = 64
SLOTS = 4
PAGES = 64
HEADS = 4
ZA, ZB, ZQ, Y, ZH, X, C = 2, 2, 2, 4, 2, 4, 2
ZL, QUAD = ZA * ZB * ZQ, ZB * ZQ
Z = ZH * ZL
LINE = ("za", "zb", "zq", "zh", "c")
N_SEQ = ZL * Y
ROWS = SLOTS * PAGE
CHUNK = 2048
SCALE = HD**-0.5 * math.log2(math.e)


def attention_kernel(counts, order, place, q_ref, own_ref, other_ref, o_ref, k_sc, v_sc):
    me = place[0]
    core = place[1]
    my_z = me // Y

    def sort_pages(k_ref, v_ref):
        def one(rank, at):
            d, j = at
            z = d // Y
            far = (z + my_z) % 2
            near = my_z + far * (1 - 2 * (my_z % 2))
            base = (d % Y) * ZL + far * (ZL // 2) + (z - near + ZL) % ZL // 2
            src = pl.multiple_of(base * ROWS + j * PAGE, PAGE)
            to = pl.multiple_of(order[rank] * PAGE, PAGE)
            k_sc[pl.ds(to, PAGE), :] = k_ref[pl.ds(src, PAGE), :]
            v_sc[pl.ds(to, PAGE), :] = v_ref[pl.ds(src, PAGE), :]
            last = j + 1 >= counts[d]
            return jnp.where(last, jnp.minimum(d + 1, N_SEQ - 1), d), jnp.where(last, 0, j + 1)

        lax.fori_loop(0, PAGES, one, (jnp.int32(0), jnp.int32(0)), unroll=PAGES)

    before = lax.fori_loop(0, me, lambda d, s: s + counts[d], jnp.int32(0))
    live = counts[me]
    head = place[2] * 2

    @pl.when((head < live) & (core == 0))
    def _():
        sort_pages(own_ref, other_ref)

    @pl.when((head < live) & (core == 1))
    def _():
        sort_pages(other_ref, own_ref)

    def store(i, rows):
        for b in range(2):
            for h in range(HEADS):
                o_ref[2 * i + b, :, h * HD : (h + 1) * HD] = rows(h, b)

    for i in range(2):
        j = head + i
        here = pl.ds(pl.multiple_of(j * PAGE, PAGE), PAGE)

        @pl.when(j < live)
        def _():
            page = order[before + j]
            q = jnp.concatenate([q_ref[here, h * HD : (h + 1) * HD] for h in range(HEADS)], axis=0)
            size = HEADS * PAGE

            def step(at, state, masked, width):
                best, total, accum = state
                k = k_sc[pl.ds(at, width), :]
                v = v_sc[pl.ds(at, width), :]
                s = lax.dot_general(q, k, (((1,), (1,)), ((), ())), preferred_element_type=jnp.float32)
                if masked:
                    row = lax.broadcasted_iota(jnp.int32, s.shape, 0) % PAGE + page * PAGE
                    seen = lax.broadcasted_iota(jnp.int32, s.shape, 1) + at <= row
                    s = jnp.where(seen, s, jnp.float32(-1e30))
                new = jnp.maximum(best, jnp.max(s, axis=1, keepdims=True))
                p = jnp.exp2((s - new) * SCALE)
                fade = jnp.exp2((best - new) * SCALE)
                total = total * fade + jnp.sum(p, axis=1, keepdims=True)
                accum = accum * fade + jnp.dot(p.astype(jnp.bfloat16), v, preferred_element_type=jnp.float32)
                return new, total, accum

            state = (
                jnp.full((size, 1), -1e30, jnp.float32),
                jnp.zeros((size, 1), jnp.float32),
                jnp.zeros((size, HD), jnp.float32),
            )
            full = page // (CHUNK // PAGE)
            state = lax.fori_loop(
                0, full, lambda i, s: step(pl.multiple_of(i * CHUNK, CHUNK), s, False, CHUNK), state
            )
            rest = pl.multiple_of(full * CHUNK, CHUNK)
            state = lax.switch(
                page % (CHUNK // PAGE) // (CHUNK // PAGE // 4),
                [lambda s, n=n: step(rest, s, True, (n + 1) * CHUNK // 4) for n in range(4)],
                state,
            )
            _, total, accum = state
            out = (accum / total).astype(jnp.bfloat16)
            store(i, lambda h, b: out[h * PAGE + b * 32 : h * PAGE + b * 32 + 32, :])

        @pl.when(j >= live)
        def _():
            store(i, lambda h, b: jnp.zeros((32, HD), jnp.bfloat16))


def attend(counts, order, place, q, own, other):
    smem = pl.BlockSpec(memory_space=pltpu.SMEM)
    vmem = pl.BlockSpec(memory_space=pltpu.VMEM)
    return pl.pallas_call(
        attention_kernel,
        out_shape=jax.ShapeDtypeStruct((X, 32, HEADS * HD), jnp.bfloat16),
        in_specs=[smem, smem, smem, vmem, vmem, vmem],
        out_specs=vmem,
        scratch_shapes=[pltpu.VMEM((PAGES * PAGE, HD), jnp.bfloat16) for _ in range(2)],
        compiler_params=pltpu.CompilerParams(vmem_limit_bytes=40 << 20),
    )(counts, order, place, q, own, other)


def project_kernel(me, a_ref, b_ref, w_ref, o_ref):
    half = a_ref.shape[-1]
    w = jnp.concatenate([w_ref[i, j] for i in range(2) for j in range(ZA)], axis=1)
    rows = jnp.concatenate([a_ref[...].reshape(-1, half), b_ref[...].reshape(-1, half)], axis=1)
    part = jnp.dot(rows, w, preferred_element_type=jnp.float32)
    part = part.astype(jnp.bfloat16).reshape(QUAD, X, 32, 4 * HD)
    for i in range(QUAD):
        o_ref[:, me[0] ^ ((QUAD - i) % QUAD)] = part[i]


def project(me, a, b, w):
    rows = pl.BlockSpec(a.shape, lambda i: (0, 0, 0, 0))
    return pl.pallas_call(
        project_kernel,
        grid=(Y // 2,),
        out_shape=jax.ShapeDtypeStruct((X, QUAD, 32, ZL * HD), jnp.bfloat16),
        in_specs=[pl.BlockSpec(memory_space=pltpu.SMEM), rows, rows, pl.BlockSpec((2, *w.shape[1:]), lambda i: (i, 0, 0, 0))],
        out_specs=pl.BlockSpec((X, QUAD, 32, 4 * HD), lambda i: (0, 0, 0, i)),
        compiler_params=pltpu.CompilerParams(vmem_limit_bytes=24 << 20),
    )(me, a, b, w)


def add_kernel(p_ref, o_ref):
    total = p_ref[0].astype(jnp.float32)
    for i in range(1, X):
        total += p_ref[i].astype(jnp.float32)
    o_ref[0] = total.astype(jnp.bfloat16)
    o_ref[1] = total.astype(jnp.bfloat16)


def add_parts(parts):
    return pl.pallas_call(
        add_kernel,
        grid=(QUAD,),
        out_shape=jax.ShapeDtypeStruct((ZH, *parts.shape[1:]), jnp.bfloat16),
        in_specs=[pl.BlockSpec((X, 1, *parts.shape[2:]), lambda i: (0, i, 0, 0))],
        out_specs=pl.BlockSpec((ZH, 1, *parts.shape[2:]), lambda i: (0, i, 0, 0)),
        compiler_params=pltpu.CompilerParams(vmem_limit_bytes=16 << 20),
    )(parts)


def spread(piece, axis, count):
    return lax.all_to_all(jnp.broadcast_to(piece[None], (count, *piece.shape)), axis, 0, 0)


def swap(piece, axis):
    return lax.ppermute(piece, axis, [(0, 1), (1, 0)])


def quad(piece, step):
    return lax.ppermute(piece, ("zb", "zq"), [(i, i ^ step) for i in range(QUAD)])


def around(piece, axis, count, shift):
    return lax.ppermute(piece, axis, [((i + shift) % count, i) for i in range(count)])


def along(piece, step):
    def place(z, c):
        return ((z % ZL) * ZH + z // ZL) * C + c

    perm = [(place(z, c), place((z + step(z, c)) % Z, c)) for z in range(Z) for c in range(C)]
    return lax.ppermute(piece, LINE, perm)


def body(counts, order, queries, keys, values, weight):
    za, zb, zq, y, zh, x, c = (lax.axis_index(name) for name in ("za", "zb", "zq", "y", "zh", "x", "c"))
    zl = (za * ZB + zb) * ZQ + zq

    def piece(step):
        owner = (zh * ZL + zl + step + Z) % Z // ZL
        head = (owner * X + x) * HD
        return jnp.where(
            c == 0,
            lax.dynamic_slice_in_dim(keys, head, HD, 1),
            lax.dynamic_slice_in_dim(values, head, HD, 1),
        )

    with jax.named_scope("cache_gather"):
        here = piece(0)
        up = along(piece(-2), lambda z, c: -2)
        down = along(piece(2), lambda z, c: 2)
        far = along(piece(8 * c - 4), lambda z, c: 8 * c - 4)
        side = along(piece(jnp.where(zq == 1, 3, -3)), lambda z, c: 3 if z % 2 else -3)
        near = jnp.concatenate([here, up, down], axis=0)
        near, weight = lax.optimization_barrier((near, weight))
        beside = swap(near, "zq")
        near = jnp.concatenate(
            [near[: 2 * ROWS], far, near[2 * ROWS :], beside[: 2 * ROWS], side, beside[2 * ROWS :]], axis=0
        )
    with jax.named_scope("weight_gather"):
        given = swap(lax.dynamic_slice_in_dim(weight, (1 - c) * HD, HD, 1), "c")
        kept = lax.dynamic_slice_in_dim(weight, c * HD, HD, 1)
        narrow = jnp.concatenate([kept, given], axis=0)
        near, narrow = lax.optimization_barrier((near, narrow))
        facing = swap(narrow, "za")
    with jax.named_scope("cache_gather"):
        own = spread(near, "y", Y).reshape(N_SEQ * ROWS, HD)
        own, narrow, facing = lax.optimization_barrier((own, narrow, facing))
        other = swap(own, "c")
    with jax.named_scope("weight_gather"):
        wide = jnp.stack([jnp.where(za == 0, narrow, facing), jnp.where(za == 0, facing, narrow)])
        wide = spread(wide, "y", Y)
    with jax.named_scope("attention"):
        heads = [
            attend(counts, order, jnp.stack([zl * Y + y, c, half]).astype(jnp.int32), queries, own, other)
            for half in (1 - zh, zh)
        ]

    def projected(mine, theirs):
        with jax.named_scope("projection"):
            here = jnp.reshape(zb * ZQ + zq, (1,)).astype(jnp.int32)
            return project(here, mine, theirs, wide)

    def part_of(parts, shift):
        return lax.dynamic_index_in_dim(parts, (x + shift) % X, 0, keepdims=False)

    def gather_rows(rows):
        return jnp.stack([rows] + [quad(rows, step) for step in range(QUAD - 1, 0, -1)])

    with jax.named_scope("rows_gather"):
        first = gather_rows(heads[0])
        first, later = lax.optimization_barrier((first, heads[1]))
        theirs = swap(first, "c")
        first, theirs, wide = lax.optimization_barrier((first, theirs, wide))
        second = gather_rows(later)
    parts = projected(first, theirs)
    with jax.named_scope("sum_x"):
        away = add_parts(lax.all_to_all(parts, "x", 0, 0))
        away, second = lax.optimization_barrier((away, second))
        theirs = swap(second, "c")
    with jax.named_scope("sum_zh"):
        back = lax.all_to_all(away, "zh", 0, 0)
        back = lax.dynamic_index_in_dim(back, 1 - zh, 0, keepdims=False)
    parts = projected(second, theirs)
    with jax.named_scope("sum_x"):
        stay = part_of(parts, 0).astype(jnp.float32)
        for shift in range(X - 1, 0, -1):
            stay += around(part_of(parts, X - shift), "x", X, shift).astype(jnp.float32)
    with jax.named_scope("columns"):
        mixed = (stay + back.astype(jnp.float32)).astype(jnp.bfloat16)
        mixed = lax.all_to_all(mixed.reshape(QUAD * C, 16, ZL * HD), ("zb", "zq", "c"), 0, 0)
        mixed = mixed.reshape(ZB, ZQ, C, 16, Y, ZA, HD).transpose(3, 5, 0, 1, 4, 2, 6)
    return mixed.reshape(16, N_SEQ * 256)


def solution(mesh):
    fine = Mesh(mesh.devices.reshape(ZA, ZB, ZQ, Y, ZH, X, C), ("za", "zb", "zq", "y", "zh", "x", "c"))
    seq, tp = ("za", "zb", "zq", "y"), ("zh", "x", "c")
    return jax.shard_map(
        body,
        mesh=fine,
        in_specs=(P(), P(), P(seq, tp), P(seq, None), P(seq, None), P(tp, seq)),
        out_specs=P((*seq, *tp), None),
        check_vma=False,
    )
```

```python
import math

import jax
import jax.numpy as jnp
from jax import lax
from jax.experimental import pallas as pl
from jax.experimental.pallas import tpu as pltpu
from jax.sharding import Mesh, PartitionSpec as P

HD = 128
PAGE = 64
SLOTS = 4
PAGES = 64
HEADS = 4
ZA, ZB, ZQ, Y, ZH, X, C = 2, 2, 2, 4, 2, 4, 2
ZL, QUAD = ZA * ZB * ZQ, ZB * ZQ
Z = ZH * ZL
LINE = ("za", "zb", "zq", "zh", "c")
N_SEQ = ZL * Y
ROWS = SLOTS * PAGE
CHUNK = 2048
SCALE = HD**-0.5 * math.log2(math.e)


def attention_kernel(counts, order, place, q_ref, own_ref, other_ref, o_ref, k_sc, v_sc):
    me = place[0]
    core = place[1]
    my_z = me // Y

    def sort_pages(k_ref, v_ref):
        def one(rank, at):
            d, j = at
            z = d // Y
            far = (z + my_z) % 2
            near = my_z + far * (1 - 2 * (my_z % 2))
            base = (d % Y) * ZL + far * (ZL // 2) + (z - near + ZL) % ZL // 2
            src = pl.multiple_of(base * ROWS + j * PAGE, PAGE)
            to = pl.multiple_of(order[rank] * PAGE, PAGE)
            k_sc[pl.ds(to, PAGE), :] = k_ref[pl.ds(src, PAGE), :]
            v_sc[pl.ds(to, PAGE), :] = v_ref[pl.ds(src, PAGE), :]
            last = j + 1 >= counts[d]
            return jnp.where(last, jnp.minimum(d + 1, N_SEQ - 1), d), jnp.where(last, 0, j + 1)

        lax.fori_loop(0, PAGES, one, (jnp.int32(0), jnp.int32(0)), unroll=PAGES)

    before = lax.fori_loop(0, me, lambda d, s: s + counts[d], jnp.int32(0))
    live = counts[me]
    head = place[2] * 2

    @pl.when((head < live) & (core == 0))
    def _():
        sort_pages(own_ref, other_ref)

    @pl.when((head < live) & (core == 1))
    def _():
        sort_pages(other_ref, own_ref)

    def store(i, rows):
        for b in range(2):
            for h in range(HEADS):
                o_ref[2 * i + b, :, h * HD : (h + 1) * HD] = rows(h, b)

    for i in range(2):
        j = head + i
        here = pl.ds(pl.multiple_of(j * PAGE, PAGE), PAGE)

        @pl.when(j < live)
        def _():
            page = order[before + j]
            q = jnp.concatenate([q_ref[here, h * HD : (h + 1) * HD] for h in range(HEADS)], axis=0)
            size = HEADS * PAGE

            def step(at, state, masked, width):
                best, total, accum = state
                k = k_sc[pl.ds(at, width), :]
                v = v_sc[pl.ds(at, width), :]
                s = lax.dot_general(q, k, (((1,), (1,)), ((), ())), preferred_element_type=jnp.float32)
                if masked:
                    row = lax.broadcasted_iota(jnp.int32, (size, 1), 0) % PAGE + (page * PAGE - at)
                    seen = lax.broadcasted_iota(jnp.int32, s.shape, 1) <= row
                    s = jnp.where(seen, s, jnp.float32(-1e30))
                new = jnp.maximum(best, jnp.max(s, axis=1, keepdims=True))
                p = jnp.exp2((s - new) * SCALE)
                fade = jnp.exp2((best - new) * SCALE)
                total = total * fade + jnp.sum(p, axis=1, keepdims=True)
                accum = accum * fade + jnp.dot(p.astype(jnp.bfloat16), v, preferred_element_type=jnp.float32)
                return new, total, accum

            state = (
                jnp.full((size, 1), -1e30, jnp.float32),
                jnp.zeros((size, 1), jnp.float32),
                jnp.zeros((size, HD), jnp.float32),
            )
            full = page // (CHUNK // PAGE)
            state = lax.fori_loop(
                0, full, lambda i, s: step(pl.multiple_of(i * CHUNK, CHUNK), s, False, CHUNK), state
            )
            rest = pl.multiple_of(full * CHUNK, CHUNK)
            state = lax.switch(
                page % (CHUNK // PAGE) // (CHUNK // PAGE // 4),
                [lambda s, n=n: step(rest, s, True, (n + 1) * CHUNK // 4) for n in range(4)],
                state,
            )
            _, total, accum = state
            out = (accum / total).astype(jnp.bfloat16)
            store(i, lambda h, b: out[h * PAGE + b * 32 : h * PAGE + b * 32 + 32, :])

        @pl.when(j >= live)
        def _():
            store(i, lambda h, b: jnp.zeros((32, HD), jnp.bfloat16))


def attend(counts, order, place, q, own, other):
    smem = pl.BlockSpec(memory_space=pltpu.SMEM)
    vmem = pl.BlockSpec(memory_space=pltpu.VMEM)
    return pl.pallas_call(
        attention_kernel,
        out_shape=jax.ShapeDtypeStruct((X, 32, HEADS * HD), jnp.bfloat16),
        in_specs=[smem, smem, smem, vmem, vmem, vmem],
        out_specs=vmem,
        scratch_shapes=[pltpu.VMEM((PAGES * PAGE, HD), jnp.bfloat16) for _ in range(2)],
        compiler_params=pltpu.CompilerParams(vmem_limit_bytes=40 << 20),
    )(counts, order, place, q, own, other)


def project_kernel(me, a_ref, b_ref, w_ref, o_ref):
    half = a_ref.shape[-1]
    w = jnp.concatenate([w_ref[i, j] for i in range(2) for j in range(ZA)], axis=1)
    rows = jnp.concatenate([a_ref[...].reshape(-1, half), b_ref[...].reshape(-1, half)], axis=1)
    part = jnp.dot(rows, w, preferred_element_type=jnp.float32)
    part = part.astype(jnp.bfloat16).reshape(QUAD, X, 32, 4 * HD)
    for i in range(QUAD):
        o_ref[:, me[0] ^ ((QUAD - i) % QUAD)] = part[i]


def project(me, a, b, w):
    rows = pl.BlockSpec(a.shape, lambda i: (0, 0, 0, 0))
    return pl.pallas_call(
        project_kernel,
        grid=(Y // 2,),
        out_shape=jax.ShapeDtypeStruct((X, QUAD, 32, ZL * HD), jnp.bfloat16),
        in_specs=[pl.BlockSpec(memory_space=pltpu.SMEM), rows, rows, pl.BlockSpec((2, *w.shape[1:]), lambda i: (i, 0, 0, 0))],
        out_specs=pl.BlockSpec((X, QUAD, 32, 4 * HD), lambda i: (0, 0, 0, i)),
        compiler_params=pltpu.CompilerParams(vmem_limit_bytes=24 << 20),
    )(me, a, b, w)


def add_kernel(p_ref, o_ref):
    total = p_ref[0].astype(jnp.float32)
    for i in range(1, X):
        total += p_ref[i].astype(jnp.float32)
    o_ref[0] = total.astype(jnp.bfloat16)
    o_ref[1] = total.astype(jnp.bfloat16)


def add_parts(parts):
    return pl.pallas_call(
        add_kernel,
        grid=(QUAD,),
        out_shape=jax.ShapeDtypeStruct((ZH, *parts.shape[1:]), jnp.bfloat16),
        in_specs=[pl.BlockSpec((X, 1, *parts.shape[2:]), lambda i: (0, i, 0, 0))],
        out_specs=pl.BlockSpec((ZH, 1, *parts.shape[2:]), lambda i: (0, i, 0, 0)),
        compiler_params=pltpu.CompilerParams(vmem_limit_bytes=16 << 20),
    )(parts)


def spread(piece, axis, count):
    return lax.all_to_all(jnp.broadcast_to(piece[None], (count, *piece.shape)), axis, 0, 0)


def swap(piece, axis):
    return lax.ppermute(piece, axis, [(0, 1), (1, 0)])


def quad(piece, step):
    return lax.ppermute(piece, ("zb", "zq"), [(i, i ^ step) for i in range(QUAD)])


def around(piece, axis, count, shift):
    return lax.ppermute(piece, axis, [((i + shift) % count, i) for i in range(count)])


def along(piece, step):
    def place(z, c):
        return ((z % ZL) * ZH + z // ZL) * C + c

    perm = [(place(z, c), place((z + step(z, c)) % Z, c)) for z in range(Z) for c in range(C)]
    return lax.ppermute(piece, LINE, perm)


def body(counts, order, queries, keys, values, weight):
    za, zb, zq, y, zh, x, c = (lax.axis_index(name) for name in ("za", "zb", "zq", "y", "zh", "x", "c"))
    zl = (za * ZB + zb) * ZQ + zq

    def piece(step):
        owner = (zh * ZL + zl + step + Z) % Z // ZL
        head = (owner * X + x) * HD
        return jnp.where(
            c == 0,
            lax.dynamic_slice_in_dim(keys, head, HD, 1),
            lax.dynamic_slice_in_dim(values, head, HD, 1),
        )

    with jax.named_scope("cache_gather"):
        here = piece(0)
        up = along(piece(-2), lambda z, c: -2)
        down = along(piece(2), lambda z, c: 2)
        far = along(piece(8 * c - 4), lambda z, c: 8 * c - 4)
        side = along(piece(jnp.where(zq == 1, 3, -3)), lambda z, c: 3 if z % 2 else -3)
        near = jnp.concatenate([here, up, down], axis=0)
        near, weight = lax.optimization_barrier((near, weight))
        beside = swap(near, "zq")
        near = jnp.concatenate(
            [near[: 2 * ROWS], far, near[2 * ROWS :], beside[: 2 * ROWS], side, beside[2 * ROWS :]], axis=0
        )
    with jax.named_scope("weight_gather"):
        given = swap(lax.dynamic_slice_in_dim(weight, (1 - c) * HD, HD, 1), "c")
        kept = lax.dynamic_slice_in_dim(weight, c * HD, HD, 1)
        narrow = jnp.concatenate([kept, given], axis=0)
        near, narrow = lax.optimization_barrier((near, narrow))
        facing = swap(narrow, "za")
    with jax.named_scope("cache_gather"):
        own = spread(near, "y", Y).reshape(N_SEQ * ROWS, HD)
        own, narrow, facing = lax.optimization_barrier((own, narrow, facing))
        other = swap(own, "c")
    with jax.named_scope("weight_gather"):
        wide = jnp.stack([jnp.where(za == 0, narrow, facing), jnp.where(za == 0, facing, narrow)])
        wide = spread(wide, "y", Y)
    with jax.named_scope("attention"):
        heads = [
            attend(counts, order, jnp.stack([zl * Y + y, c, half]).astype(jnp.int32), queries, own, other)
            for half in (1 - zh, zh)
        ]

    def projected(mine, theirs):
        with jax.named_scope("projection"):
            here = jnp.reshape(zb * ZQ + zq, (1,)).astype(jnp.int32)
            return project(here, mine, theirs, wide)

    def part_of(parts, shift):
        return lax.dynamic_index_in_dim(parts, (x + shift) % X, 0, keepdims=False)

    def gather_rows(rows):
        return jnp.stack([rows] + [quad(rows, step) for step in range(QUAD - 1, 0, -1)])

    with jax.named_scope("rows_gather"):
        first = gather_rows(heads[0])
        first, later = lax.optimization_barrier((first, heads[1]))
        theirs = swap(first, "c")
        first, theirs, wide = lax.optimization_barrier((first, theirs, wide))
        second = gather_rows(later)
    parts = projected(first, theirs)
    with jax.named_scope("sum_x"):
        away = add_parts(lax.all_to_all(parts, "x", 0, 0))
        away, second = lax.optimization_barrier((away, second))
        theirs = swap(second, "c")
    with jax.named_scope("sum_zh"):
        back = lax.all_to_all(away, "zh", 0, 0)
        back = lax.dynamic_index_in_dim(back, 1 - zh, 0, keepdims=False)
    parts = projected(second, theirs)
    with jax.named_scope("sum_x"):
        stay = part_of(parts, 0).astype(jnp.float32)
        for shift in range(X - 1, 0, -1):
            stay += around(part_of(parts, X - shift), "x", X, shift).astype(jnp.float32)
    with jax.named_scope("columns"):
        mixed = (stay + back.astype(jnp.float32)).astype(jnp.bfloat16)
        mixed = lax.all_to_all(mixed.reshape(QUAD * C, 16, ZL * HD), ("zb", "zq", "c"), 0, 0)
        mixed = mixed.reshape(ZB, ZQ, C, 16, Y, ZA, HD).transpose(3, 5, 0, 1, 4, 2, 6)
    return mixed.reshape(16, N_SEQ * 256)


def solution(mesh):
    fine = Mesh(mesh.devices.reshape(ZA, ZB, ZQ, Y, ZH, X, C), ("za", "zb", "zq", "y", "zh", "x", "c"))
    seq, tp = ("za", "zb", "zq", "y"), ("zh", "x", "c")
    return jax.shard_map(
        body,
        mesh=fine,
        in_specs=(P(), P(), P(seq, tp), P(seq, None), P(seq, None), P(tp, seq)),
        out_specs=P((*seq, *tp), None),
        check_vma=False,
    )
```
